32 devices in a mesh: space: 4 (over z), block: 8 (over y, x, core).
Axes of the slice: x: 2, y: 2, z: 4, core: 2. Of those that a mesh axis runs over, the one named last changes fastest.
Arguments:
- start_vectors: float32 [256, 16, 9216], P('block', 'space'), may hold values from -210 to 210, as said below
- phase_labels: int32 [16, 9216], P('space'), may hold values from 0 to 2
- phase_conductivity: float32 [3], replicated, may hold values from 0.3 to 3
Outputs:
- basis: float32 [256, 16, 9216], P('block', 'space')
The draws below stay inside these ranges and needn't reach their ends.
Inputs may be any that keep to these rules, and one draw needn't show every extreme that they name: `start_vectors`: Real-valued starting vectors.
All inputs are finite; a program needn't handle non-finite values.
Results may differ from the reference program's by a relative error of at most 0.0003.
Values sent between devices are 32-bit elements; how exact they have to be, the bound alone decides.
No kernel may reach another device: no remote copies, remote signals or barrier semaphores. Data moves between devices by JAX's collectives and lax.ppermute only.
A program may use at most 128 MiB of HBM per device.

```python
import math
import jax
import jax.numpy as jnp
from jax import lax

M = 256
NY = 96
NZ = 96
DEGREE = 4
NX = 16


def draw_start_vectors(key, part):
    key_values, key_scales = jax.random.split(jax.random.fold_in(key, 7))
    scales = jnp.exp(jnp.log(10.0) * jax.random.uniform(key_scales, (M, 1, 1), jnp.float32))
    position = jnp.arange(NX, dtype=jnp.float32) / max(NX - 1, 1)
    values = jnp.clip(jax.random.normal(key_values, (M, NX, NY * NZ), jnp.float32), -5.0, 5.0)
    rising = 1.0 + 2.0 * position
    return (values * scales * rising[None, :, None]).astype(jnp.float32)


def place_ends(entries, stream_key, smallest, high):
    longest = entries.shape.index(max(entries.shape))
    spots = []
    for shift in (0, 1):
        where = [jax.random.randint(jax.random.fold_in(stream_key, axis), (), 0, length) for axis, length in enumerate(entries.shape)]
        where[longest] = (where[longest] + shift) % entries.shape[longest]
        spots.append(tuple(where))
    return entries.at[spots[0]].set(smallest).at[spots[1]].set(high)


def setup_inputs(seed: int = 0) -> dict:
    key_list = jax.random.split(jax.random.key(seed), 4)
    start_vectors = draw_start_vectors(jax.random.fold_in(key_list[3], 71), 0)
    phase_labels = place_ends(jax.random.randint(key_list[1], (NX, NY * NZ), 0, 3), jax.random.fold_in(key_list[1], 1), 0, 2).astype(jnp.int32)
    phase_conductivity = jnp.clip(jnp.exp(jax.random.uniform(key_list[2], (3,), jnp.float32, math.log(0.3), math.log(3.0))), 0.3, 3.0)
    return {"start_vectors": start_vectors, "phase_labels": phase_labels, "phase_conductivity": phase_conductivity}


def plane_shift(field, offset):
    length = field.shape[-1]
    widths = [(0, 0)] * (field.ndim - 1)
    if offset > 0:
        return jnp.pad(field, widths + [(0, offset)])[..., offset:]
    return jnp.pad(field, widths + [(-offset, 0)])[..., :length]

def harmonic(left_k, right_k):
    filled = jnp.where(right_k > 0, right_k, left_k)
    return 2.0 * left_k * filled / (left_k + filled)

def conductances(extended, depth):
    center_k = extended[1:-1]
    z_index = jnp.arange(center_k.shape[-1]) % depth
    face_list = [harmonic(center_k, extended[:-2]), harmonic(center_k, extended[2:])]
    for offset in (1, -1, depth, -depth):
        nearby = plane_shift(center_k, offset)
        if offset == 1:
            nearby = jnp.where(z_index < depth - 1, nearby, 0.0)
        if offset == -1:
            nearby = jnp.where(z_index > 0, nearby, 0.0)
        face_list.append(harmonic(center_k, nearby))
    return face_list

def apply_operator(extended, face_list, depth):
    field = extended[:, 1:-1]
    z_index = jnp.arange(field.shape[-1]) % depth
    z_upper = (z_index < depth - 1).astype(jnp.float32)
    z_lower = (z_index > 0).astype(jnp.float32)
    summed = face_list[0] * (field - extended[:, :-2]) + face_list[1] * (field - extended[:, 2:])
    for place, offset in enumerate((1, -1, depth, -depth)):
        nearby = plane_shift(field, offset)
        if offset == 1:
            nearby = nearby * z_upper
        if offset == -1:
            nearby = nearby * z_lower
        summed = summed + face_list[2 + place] * (field - nearby)
    return summed

def reference(start_vectors, phase_labels, phase_conductivity):
    table = phase_conductivity
    conduct = jnp.where(phase_labels == 0, table[0], jnp.where(phase_labels == 1, table[1], table[2])).astype(jnp.float32)
    face_list = conductances(jnp.pad(conduct, ((1, 1), (0, 0))), NZ)
    upper_bound = 12.0 * jnp.max(table)
    lower_bound = upper_bound / 10.0
    centre = (upper_bound + lower_bound) / 2.0
    radius = (upper_bound - lower_bound) / 2.0

    def operate(field):
        return apply_operator(jnp.pad(field, ((0, 0), (1, 1), (0, 0))), face_list, NZ)
    before = start_vectors
    current = (operate(before) - centre * before) / radius
    for degree_step in range(DEGREE - 1):
        following = 2.0 * (operate(current) - centre * current) / radius - before
        before, current = (current, following)
    cells = NX * NY * NZ
    rows = current.reshape(M, cells)
    split = M // 2
    first, second = (rows[:split], rows[split:])

    def inner(left, right):
        return jnp.dot(left, right.T, precision=lax.Precision.HIGHEST) / cells
    lower_one = jnp.linalg.cholesky(inner(first, first))
    basis_one = jax.scipy.linalg.solve_triangular(lower_one, first, lower=True)
    coupling = inner(basis_one, second)
    remainder = second - jnp.dot(coupling.T, basis_one, precision=lax.Precision.HIGHEST)
    lower_two = jnp.linalg.cholesky(inner(remainder, remainder))
    basis_two = jax.scipy.linalg.solve_triangular(lower_two, remainder, lower=True)
    return jnp.concatenate([basis_one, basis_two], 0).reshape(M, NX, NY * NZ)
```

```python
import functools

import jax
import jax.numpy as jnp
from jax import lax
from jax.experimental import pallas as pl
from jax.experimental.pallas import tpu as pltpu
from jax.sharding import PartitionSpec as P

NZ = 96
DEGREE = 4
LANES = 128
CHUNK = 8
TERMS = 8
HIGHEST = lax.Precision.HIGHEST


def neighbours(axis):
    count = lax.axis_size(axis)
    up = [(i, i + 1) for i in range(count - 1)]
    return up, [(b, a) for a, b in up]


def plane_shift(field, offset):
    length = field.shape[-1]
    widths = [(0, 0)] * (field.ndim - 1)
    if offset > 0:
        return jnp.pad(field, widths + [(0, offset)])[..., offset:]
    return jnp.pad(field, widths + [(-offset, 0)])[..., :length]


def harmonic(left_k, right_k):
    filled = jnp.where(right_k > 0, right_k, left_k)
    return 2.0 * left_k * filled / (left_k + filled)


def lookup(labels, table):
    return jnp.where(labels == 0, table[0], jnp.where(labels == 1, table[1], table[2]))


def stencil_terms(rimmed, centre, radius):
    kappa = rimmed[1:-1]
    inside = kappa > 0
    safe = jnp.where(inside, kappa, 1.0)
    z_index = jnp.arange(kappa.shape[-1]) % NZ
    around = [rimmed[:-2], rimmed[2:]]
    for offset in (1, -1, NZ, -NZ):
        nearby = plane_shift(kappa, offset)
        if offset == 1:
            nearby = jnp.where(z_index < NZ - 1, nearby, 0.0)
        if offset == -1:
            nearby = jnp.where(z_index > 0, nearby, 0.0)
        around.append(nearby)
    scale = 2.0 / radius
    faces = [harmonic(safe, k) for k in around]
    diagonal = functools.reduce(jnp.add, faces) - centre
    rows = [jnp.where(inside, diagonal * scale, 0.0)]
    for face, k in zip(faces, around):
        rows.append(jnp.where(inside & (k > 0), -scale * face, 0.0))
    rows.append(jnp.zeros_like(kappa))
    return jnp.stack(rows, axis=1)


def filter_kernel(planes, halves, low, own, high, terms, out, y0, y1, y2, y3, sems):
    copies = [
        pltpu.make_async_copy(source, y0.at[pl.ds(k * planes, planes)], sems.at[k])
        for k, source in enumerate((low, own, high))
    ]
    for copy in copies:
        copy.start()
    for copy in copies:
        copy.wait()
    cells = y0.shape[-1]
    tiles = cells // LANES
    per_half = tiles // halves
    group = next(g for g in (9, 6, 4, 3, 2, 1) if per_half % g == 0)
    lane = lax.broadcasted_iota(jnp.int32, (CHUNK, LANES), 1)
    last, first = lane == LANES - 1, lane == 0
    head, tail = lane < LANES - NZ % LANES, lane >= NZ % LANES

    def sweep(source, source_at, previous, previous_at, target, at, half_step):
        count = target_planes(target)

        def plane_body(p, carry):
            w = p + at

            def group_body(g, carry):
                t0 = g * group
                s = source_at(w)

                def tile(plane, t):
                    return source[plane, :, pl.ds(pl.multiple_of(t * LANES, LANES), LANES)]

                before = jnp.where(t0 == 0, tiles - 1, t0 - 1)
                after = jnp.where(t0 + group == tiles, 0, t0 + group)
                row = [tile(s, before)] + [tile(s, t0 + i) for i in range(group)] + [tile(s, after)]
                down = [pltpu.roll(v, LANES - 1, 1) for v in row[1:]]
                up = [pltpu.roll(v, 1, 1) for v in row[:-1]]
                ahead = [pltpu.roll(v, LANES - NZ, 1) for v in row[1:]]
                behind = [pltpu.roll(v, NZ, 1) for v in row[:-1]]
                for i in range(group):
                    lanes = pl.ds(pl.multiple_of((t0 + i) * LANES, LANES), LANES)

                    def term(k):
                        return terms[w - 1, pl.ds(k, 1), lanes]

                    total = term(0) * row[i + 1]
                    total += term(1) * tile(s - 1, t0 + i)
                    total += term(2) * tile(s + 1, t0 + i)
                    total += term(3) * jnp.where(last, down[i + 1], down[i])
                    total += term(4) * jnp.where(first, up[i], up[i + 1])
                    total += term(5) * jnp.where(head, ahead[i], ahead[i + 1])
                    total += term(6) * jnp.where(tail, behind[i + 1], behind[i])
                    if half_step:
                        total = 0.5 * total
                    else:
                        total -= previous[previous_at(w), :, lanes]
                    if target is out:
                        half = lax.div(t0, per_half)
                        inner = pl.multiple_of((t0 + i - half * per_half) * LANES, LANES)
                        out[p * halves + half, :, pl.ds(inner, LANES)] = total
                    else:
                        target[p, :, lanes] = total
                return carry

            return lax.fori_loop(0, tiles // group, group_body, carry)

        lax.fori_loop(0, count, plane_body, 0)

    def target_planes(target):
        return planes if target is out else target.shape[0]

    sweep(y0, lambda w: w, None, None, y1, 1, True)
    sweep(y1, lambda w: w - 1, y0, lambda w: w, y2, 2, False)
    sweep(y2, lambda w: w - 2, y1, lambda w: w - 1, y3, 3, False)
    sweep(y3, lambda w: w - 3, y2, lambda w: w - 2, out, 4, False)


def filtered(low, own, high, terms, blocks):
    planes, rows, cells = own.shape
    halves = blocks // planes
    width = cells // halves
    window = 3 * planes
    steps = (3 * planes - 2, 3 * planes - 4, 3 * planes - 6)
    anywhere = pl.BlockSpec(memory_space=pl.ANY)
    return pl.pallas_call(
        functools.partial(filter_kernel, planes, halves),
        out_shape=jax.ShapeDtypeStruct((blocks, rows, width), jnp.float32),
        in_specs=[anywhere] * 3 + [pl.BlockSpec(memory_space=pltpu.VMEM)],
        out_specs=pl.BlockSpec(memory_space=pltpu.VMEM),
        scratch_shapes=[pltpu.VMEM((window, rows, cells), jnp.float32)]
        + [pltpu.VMEM((count, rows, cells), jnp.float32) for count in steps]
        + [pltpu.SemaphoreType.DMA((3,))],
        compiler_params=pltpu.CompilerParams(vmem_limit_bytes=24 * 2**20),
        cost_estimate=pl.CostEstimate(
            flops=14 * 7 * planes * rows * cells,
            bytes_accessed=4 * (window + planes + 20) * rows * cells,
            transcendentals=0,
        ),
        name="chebyshev",
    )(low, own, high, terms)


def local(start_vectors, phase_labels, phase_conductivity):
    upper_bound = 12.0 * jnp.max(phase_conductivity)
    lower_bound = upper_bound / 10.0
    centre = (upper_bound + lower_bound) / 2.0
    radius = (upper_bound - lower_bound) / 2.0
    per_device, planes, plane_cells = start_vectors.shape
    blocks, slabs = lax.axis_size("block"), lax.axis_size("space")
    assert planes == DEGREE and blocks % planes == 0
    halves = blocks // planes
    width = plane_cells // halves
    cells = planes * slabs * plane_cells
    rank = per_device * blocks
    up, back = neighbours("space")
    chunks = per_device // CHUNK

    conduct = lookup(phase_labels, phase_conductivity)
    rimmed = jnp.concatenate(
        [lax.ppermute(conduct, "space", up), conduct, lax.ppermute(conduct, "space", back)], axis=0
    )
    terms = stencil_terms(rimmed, centre, radius)

    received = []
    for c in range(chunks):
        own = jnp.swapaxes(start_vectors[c * CHUNK : (c + 1) * CHUNK], 0, 1)
        low = lax.ppermute(own, "space", up)
        high = lax.ppermute(own, "space", back)
        part = filtered(low, own, high, terms, blocks)
        received.append(lax.all_to_all(part, "block", 0, 0, tiled=True))
    field = jnp.stack(received, axis=1).reshape(rank, width)

    partial = jnp.einsum("mp,np->mn", field, field, precision=HIGHEST)
    devices = blocks * slabs
    pieces = partial.reshape(devices, rank // devices, rank)
    summed = jnp.sum(lax.all_to_all(pieces, ("space", "block"), 0, 0, tiled=True), axis=0)
    gram = lax.all_to_all(
        jnp.broadcast_to(summed[None], pieces.shape), ("space", "block"), 0, 0, tiled=True
    ).reshape(rank, rank)
    lower_factor = jnp.linalg.cholesky(gram / cells)
    inverse = jax.scipy.linalg.solve_triangular(
        lower_factor, jnp.eye(rank, dtype=jnp.float32), lower=True
    )
    result = jnp.einsum("mn,np->mp", inverse, field, precision=HIGHEST)
    sent = lax.all_to_all(result.reshape(blocks, per_device, width), "block", 0, 0, tiled=True)
    return sent.reshape(planes, halves, per_device, width).transpose(2, 0, 1, 3).reshape(
        per_device, planes, plane_cells
    )


def solution(mesh):
    return jax.shard_map(
        local,
        mesh=mesh,
        in_specs=(P("block", "space", None), P("space", None), P()),
        out_specs=P("block", "space", None),
        check_vma=False,
    )
```

```python
import functools
import math

import jax
import jax.numpy as jnp
from jax import lax
from jax.experimental import pallas as pl
from jax.experimental.pallas import tpu as pltpu
from jax.sharding import PartitionSpec as P

NZ = 96
DEGREE = 4
LANES = 128
CHUNK = 8
PANEL = 32
HIGHEST = lax.Precision.HIGHEST


def neighbours(axis):
    count = lax.axis_size(axis)
    up = [(i, i + 1) for i in range(count - 1)]
    return up, [(b, a) for a, b in up]


def lookup(labels, table):
    return jnp.where(labels == 0, table[0], jnp.where(labels == 1, table[1], table[2]))


def face(left_k, right_k):
    filled = jnp.where(right_k > 0, right_k, left_k)
    return 2.0 * left_k * filled / (left_k + filled)


def terms_kernel(planes, scales, low, own, high, out, window):
    scale, shift = scales[0], scales[1]
    count = out.shape[0]
    window[...] = jnp.zeros_like(window)
    for k, source in enumerate((low, own, high)):
        window[k * planes : (k + 1) * planes, :] = source[0]
    cells = window.shape[1]
    span = 3 * LANES * NZ // math.gcd(3 * LANES, NZ)
    assert cells % span == 0
    z = lax.rem(lax.broadcasted_iota(jnp.int32, (8, span), 1), NZ)

    def body(g, carry):
        lanes = pl.ds(pl.multiple_of(g * span, span), span)
        left = pl.ds(pl.multiple_of(jnp.maximum(g * span - LANES, 0), LANES), LANES)
        right = pl.ds(
            pl.multiple_of(jnp.minimum(g * span + span, cells - LANES), LANES), LANES
        )
        for base in range(0, count, 8):
            rows = pl.ds(base + 1, 8)
            kappa = window[rows, lanes]
            inside = kappa > 0
            safe = jnp.where(inside, kappa, 1.0)
            before = jnp.where(g == 0, 0.0, window[rows, left])
            after = jnp.where(g * span + span == cells, 0.0, window[rows, right])
            wide = jnp.concatenate([before, kappa, after], axis=1)
            total = wide.shape[1]

            def moved(offset):
                return pltpu.roll(wide, (-offset) % total, 1)[:, LANES : LANES + span]

            around = [
                window[pl.ds(base, 8), lanes],
                window[pl.ds(base + 2, 8), lanes],
                jnp.where(z < NZ - 1, moved(1), 0.0),
                jnp.where(z > 0, moved(-1), 0.0),
                moved(NZ),
                moved(-NZ),
            ]
            faces = [face(safe, k) for k in around]
            diagonal = functools.reduce(jnp.add, faces) - shift
            values = [jnp.where(inside, diagonal * scale, 0.0)]
            for f, k in zip(faces, around):
                values.append(jnp.where(inside & (k > 0), -scale * f, 0.0))
            kept = min(8, count - base)
            for k, value in enumerate(values):
                out[base : base + kept, k, lanes] = value[:kept]
        return carry

    lax.fori_loop(0, cells // span, body, 0)


def stencil_terms(low, own, high, centre, radius):
    planes, cells = own.shape[1:]
    inner = 3 * planes - 2
    smem, vmem = pl.BlockSpec(memory_space=pltpu.SMEM), pl.BlockSpec(memory_space=pltpu.VMEM)
    return pl.pallas_call(
        functools.partial(terms_kernel, planes),
        out_shape=jax.ShapeDtypeStruct((inner, 8, cells), jnp.float32),
        in_specs=[smem] + [vmem] * 3,
        out_specs=vmem,
        scratch_shapes=[pltpu.VMEM((24, cells), jnp.float32)],
        compiler_params=pltpu.CompilerParams(vmem_limit_bytes=24 * 2**20),
        name="stencil_terms",
    )(jnp.stack([2.0 / radius, centre]), low, own, high)


def filter_kernel(planes, halves, low, own, high, terms, out, y0, y1, y2, y3):
    for k, source in enumerate((low, own, high)):
        for p in range(planes):
            y0[k * planes + p] = source[0:CHUNK, p, :]
    cells = y0.shape[-1]
    tiles = cells // LANES
    per_half = tiles // halves
    group = per_half
    lane = lax.broadcasted_iota(jnp.int32, (CHUNK, LANES), 1)
    last, first = lane == LANES - 1, lane == 0
    head, tail = lane < NZ, lane >= LANES - NZ

    def sweep(source, source_at, previous, previous_at, target, at, half_step):
        count = target_planes(target)

        def plane_body(p, carry):
            w = p + at

            def group_body(g, carry):
                t0 = g * group
                s = source_at(w)
                span = pl.ds(pl.multiple_of(t0 * LANES, LANES), group * LANES)
                before = jnp.where(t0 == 0, tiles - 1, t0 - 1)
                after = jnp.where(t0 + group == tiles, 0, t0 + group)

                def edge(t):
                    return source[s, :, pl.ds(pl.multiple_of(t * LANES, LANES), LANES)]

                def cut(wide):
                    return [wide[:, i * LANES : (i + 1) * LANES] for i in range(group)]

                row = [edge(before)] + cut(source[s, :, span]) + [edge(after)]
                below, above = cut(source[s - 1, :, span]), cut(source[s + 1, :, span])
                rows = [cut(terms[w - 1, pl.ds(k, 1), span]) for k in range(7)]
                if not half_step:
                    older = cut(previous[previous_at(w), :, span])
                results = []
                for i in range(group):
                    left, here, right = row[i : i + 3]
                    total = rows[0][i] * here
                    total += rows[1][i] * below[i]
                    total += rows[2][i] * above[i]
                    total += rows[3][i] * pltpu.roll(jnp.where(first, right, here), LANES - 1, 1)
                    total += rows[4][i] * pltpu.roll(jnp.where(last, left, here), 1, 1)
                    total += rows[5][i] * pltpu.roll(jnp.where(head, right, here), LANES - NZ, 1)
                    total += rows[6][i] * pltpu.roll(jnp.where(tail, left, here), NZ, 1)
                    results.append(0.5 * total if half_step else total - older[i])
                result = jnp.concatenate(results, axis=1)
                if target is out:
                    half = lax.div(t0, per_half)
                    inner = pl.multiple_of((t0 - half * per_half) * LANES, LANES)
                    out[p * halves + half, :, pl.ds(inner, group * LANES)] = result
                else:
                    target[p, :, span] = result
                return carry

            return lax.fori_loop(0, tiles // group, group_body, carry, unroll=True)

        lax.fori_loop(0, count, plane_body, 0)

    def target_planes(target):
        return planes if target is out else target.shape[0]

    sweep(y0, lambda w: w, None, None, y1, 1, True)
    sweep(y1, lambda w: w - 1, y0, lambda w: w, y2, 2, False)
    sweep(y2, lambda w: w - 2, y1, lambda w: w - 1, y3, 3, False)
    sweep(y3, lambda w: w - 3, y2, lambda w: w - 2, out, 4, False)


def filtered(low, own, high, terms, blocks):
    planes, cells = own.shape[1:]
    halves = blocks // planes
    width = cells // halves
    steps = (3 * planes, 3 * planes - 2, 3 * planes - 4, 3 * planes - 6)
    vmem = pl.BlockSpec(memory_space=pltpu.VMEM)
    return pl.pallas_call(
        functools.partial(filter_kernel, planes, halves),
        out_shape=jax.ShapeDtypeStruct((blocks, CHUNK, width), jnp.float32),
        in_specs=[vmem] * 4,
        out_specs=vmem,
        scratch_shapes=[pltpu.VMEM((count, CHUNK, cells), jnp.float32) for count in steps],
        compiler_params=pltpu.CompilerParams(vmem_limit_bytes=32 * 2**20),
        cost_estimate=pl.CostEstimate(
            flops=14 * 7 * planes * CHUNK * cells,
            bytes_accessed=4 * 44 * CHUNK * cells,
            transcendentals=0,
        ),
        name="chebyshev",
    )(low, own, high, terms)


def assemble_kernel(planes, source, out):
    for m in range(0, out.shape[0], 8):
        for p in range(planes):
            out[m : m + 8, p, :] = source[p, 0, m : m + 8, :]


def assembled(pieces):
    planes, halves, rows, width = pieces.shape
    return pl.pallas_call(
        functools.partial(assemble_kernel, planes),
        grid=(halves,),
        out_shape=jax.ShapeDtypeStruct((rows, planes, halves * width), jnp.float32),
        in_specs=[pl.BlockSpec((planes, 1, rows, width), lambda i: (0, i, 0, 0))],
        out_specs=pl.BlockSpec((rows, planes, width), lambda i: (0, 0, i)),
        compiler_params=pltpu.CompilerParams(vmem_limit_bytes=32 * 2**20),
        name="assemble",
    )(pieces)


def inverse_factor_kernel(scale, gram, out, work):
    rank = gram.shape[0]
    work[...] = gram[...] * scale
    lane = lax.broadcasted_iota(jnp.int32, (8, rank), 1)
    sub = lax.broadcasted_iota(jnp.int32, (8, 1), 0)
    for k0 in range(0, rank, PANEL):
        groups = [work[k0 + 8 * g : k0 + 8 * g + 8, :] for g in range(PANEL // 8)]
        pivots = [jnp.ones((8, 1), jnp.float32)] * len(groups)
        for j in range(PANEL):
            at, inner, column = j // 8, j % 8, k0 + j
            here = lane == column
            pivot = groups[at][inner : inner + 1, column : column + 1]
            inverse = 1.0 / pivot
            pivots[at] = jnp.where(sub == inner, pivot, pivots[at])
            row = jnp.where(here[:1], 1.0, groups[at][inner : inner + 1, :]) * inverse
            for g in range(at, len(groups)):
                factor = groups[g][:, column : column + 1]
                if g == at:
                    factor = jnp.where(sub > inner, factor, 0.0)
                    kept = jnp.where(here, jnp.where(sub == inner, 1.0, 0.0), groups[g])
                    if inner:
                        kept = jnp.where(sub < inner, groups[g], kept)
                else:
                    kept = jnp.where(here, 0.0, groups[g])
                groups[g] = kept - factor * row
        scaled = [v / jnp.sqrt(p) for v, p in zip(groups, pivots)]
        panel = jnp.concatenate(scaled, axis=0)
        done = k0 + PANEL
        columns = lax.broadcasted_iota(jnp.int32, (PANEL, rank), 1)
        rows = k0 + lax.broadcasted_iota(jnp.int32, (PANEL, rank), 0)
        behind = columns <= rows
        out[k0:done, :] = jnp.where(behind, panel, 0.0)
        panel = jnp.where(behind | (columns >= done), panel, 0.0)
        if done < rank:
            update = lax.dot_general(
                panel, panel, (((0,), (0,)), ((), ())), precision=HIGHEST,
                preferred_element_type=jnp.float32,
            )
            inside = (columns[:1] >= k0) & (columns[:1] < done)
            work[done:, :] = jnp.where(inside, 0.0, work[done:, :]) - update[done:, :]


def inverse_factor(gram, scale):
    rank = gram.shape[0]
    return pl.pallas_call(
        functools.partial(inverse_factor_kernel, scale),
        out_shape=jax.ShapeDtypeStruct((rank, rank), jnp.float32),
        in_specs=[pl.BlockSpec(memory_space=pltpu.VMEM)],
        out_specs=pl.BlockSpec(memory_space=pltpu.VMEM),
        scratch_shapes=[pltpu.VMEM((rank, rank), jnp.float32)],
        name="inverse_factor",
    )(gram)


def local(start_vectors, phase_labels, phase_conductivity):
    upper_bound = 12.0 * jnp.max(phase_conductivity)
    lower_bound = upper_bound / 10.0
    centre = (upper_bound + lower_bound) / 2.0
    radius = (upper_bound - lower_bound) / 2.0
    per_device, planes, plane_cells = start_vectors.shape
    blocks, slabs = lax.axis_size("block"), lax.axis_size("space")
    assert planes == DEGREE and blocks % planes == 0
    halves = blocks // planes
    width = plane_cells // halves
    cells = planes * slabs * plane_cells
    rank = per_device * blocks
    up, back = neighbours("space")
    chunks = per_device // CHUNK

    conduct = lookup(phase_labels, phase_conductivity)
    received = []
    for c in range(chunks):
        own = start_vectors[c * CHUNK : (c + 1) * CHUNK]
        if c == 0:
            own = jnp.concatenate([own, conduct[None]], axis=0)
        low = lax.ppermute(own, "space", up)
        high = lax.ppermute(own, "space", back)
        if c == 0:
            terms = stencil_terms(
                low[CHUNK:], conduct[None], high[CHUNK:], centre, radius
            )
        part = filtered(low, own, high, terms, blocks)
        received.append(lax.all_to_all(part, "block", 0, 0, tiled=True))
    field = jnp.stack(received, axis=1).reshape(rank, width)

    partial = jnp.einsum("mp,np->mn", field, field, precision=HIGHEST)
    devices = blocks * slabs
    pieces = partial.reshape(devices, rank // devices, rank)
    summed = jnp.sum(lax.all_to_all(pieces, ("space", "block"), 0, 0, tiled=True), axis=0)
    gram = lax.all_to_all(
        jnp.broadcast_to(summed[None], pieces.shape), ("space", "block"), 0, 0, tiled=True
    ).reshape(rank, rank)
    inverse = inverse_factor(gram, 1.0 / cells)
    result = jnp.einsum("mn,np->mp", inverse, field, precision=HIGHEST)
    sent = lax.all_to_all(result.reshape(blocks, per_device, width), "block", 0, 0, tiled=True)
    return assembled(sent.reshape(planes, halves, per_device, width))


def solution(mesh):
    return jax.shard_map(
        local,
        mesh=mesh,
        in_specs=(P("block", "space", None), P("space", None), P()),
        out_specs=P("block", "space", None),
        check_vma=False,
    )
```

```python
import functools
import math

import jax
import jax.numpy as jnp
from jax import lax
from jax.experimental import pallas as pl
from jax.experimental.pallas import tpu as pltpu
from jax.sharding import PartitionSpec as P

NZ = 96
DEGREE = 4
LANES = 128
CHUNK = 8
PANEL = 64
BLOCK = 9 * LANES
HIGHEST = lax.Precision.HIGHEST


def neighbours(axis):
    count = lax.axis_size(axis)
    up = [(i, i + 1) for i in range(count - 1)]
    return up, [(b, a) for a, b in up]


def first_chunk_kernel(table, labels, vectors, out):
    out[0:CHUNK] = vectors[...]
    phase = labels[...]
    out[CHUNK] = jnp.where(phase == 0, table[0], jnp.where(phase == 1, table[1], table[2]))


def first_chunk(vectors, labels, table):
    planes, cells = labels.shape
    return pl.pallas_call(
        first_chunk_kernel,
        grid=(1,),
        out_shape=jax.ShapeDtypeStruct((CHUNK + 1, planes, cells), jnp.float32),
        in_specs=[
            pl.BlockSpec(memory_space=pltpu.SMEM),
            pl.BlockSpec((planes, cells), lambda i: (0, 0)),
            pl.BlockSpec((CHUNK, planes, cells), lambda i: (0, 0, 0)),
        ],
        out_specs=pl.BlockSpec((CHUNK + 1, planes, cells), lambda i: (0, 0, 0)),
        name="first_chunk",
    )(table, labels, vectors)


def face(left_k, right_k):
    filled = jnp.where(right_k > 0, right_k, left_k)
    return 2.0 * left_k * filled / (left_k + filled)


def terms_kernel(planes, scales, low, own, high, out, window):
    scale, shift = scales[0], scales[1]
    count = out.shape[0]
    window[...] = jnp.zeros_like(window)
    for k, source in enumerate((low, own, high)):
        window[k * planes : (k + 1) * planes, :] = source[CHUNK]
    cells = window.shape[1]
    span = 3 * LANES * NZ // math.gcd(3 * LANES, NZ)
    assert cells % span == 0
    z = lax.rem(lax.broadcasted_iota(jnp.int32, (8, span), 1), NZ)

    def body(g, carry):
        lanes = pl.ds(pl.multiple_of(g * span, span), span)
        left = pl.ds(pl.multiple_of(jnp.maximum(g * span - LANES, 0), LANES), LANES)
        right = pl.ds(
            pl.multiple_of(jnp.minimum(g * span + span, cells - LANES), LANES), LANES
        )
        for base in range(0, count, 8):
            rows = pl.ds(base + 1, 8)
            kappa = window[rows, lanes]
            inside = kappa > 0
            safe = jnp.where(inside, kappa, 1.0)
            before = jnp.where(g == 0, 0.0, window[rows, left])
            after = jnp.where(g * span + span == cells, 0.0, window[rows, right])
            wide = jnp.concatenate([before, kappa, after], axis=1)
            total = wide.shape[1]

            def moved(offset):
                return pltpu.roll(wide, (-offset) % total, 1)[:, LANES : LANES + span]

            around = [
                window[pl.ds(base, 8), lanes],
                window[pl.ds(base + 2, 8), lanes],
                jnp.where(z < NZ - 1, moved(1), 0.0),
                jnp.where(z > 0, moved(-1), 0.0),
                moved(NZ),
                moved(-NZ),
            ]
            faces = [face(safe, k) for k in around]
            diagonal = functools.reduce(jnp.add, faces) - shift
            values = [jnp.where(inside, diagonal * scale, 0.0)]
            for f, k in zip(faces, around):
                values.append(jnp.where(inside & (k > 0), -scale * f, 0.0))
            kept = min(8, count - base)
            for k, value in enumerate(values):
                out[base : base + kept, k, lanes] = value[:kept]
        return carry

    lax.fori_loop(0, cells // span, body, 0)


def filter_kernel(planes, halves, low, own, high, terms, out, y0, y1, y2, y3):
    for k, source in enumerate((low, own, high)):
        for p in range(planes):
            y0[k * planes + p] = source[0:CHUNK, p, :]
    cells = y0.shape[-1]
    tiles = cells // LANES
    per_half = tiles // halves
    group = per_half
    lane = lax.broadcasted_iota(jnp.int32, (CHUNK, LANES), 1)
    last, first = lane == LANES - 1, lane == 0
    head, tail = lane < NZ, lane >= LANES - NZ

    def sweep(source, source_at, previous, previous_at, target, at, half_step):
        count = target_planes(target)

        def plane_body(p, carry):
            w = p + at

            def group_body(g, carry):
                t0 = g * group
                s = source_at(w)
                span = pl.ds(pl.multiple_of(t0 * LANES, LANES), group * LANES)
                before = jnp.where(t0 == 0, tiles - 1, t0 - 1)
                after = jnp.where(t0 + group == tiles, 0, t0 + group)

                def edge(t):
                    return source[s, :, pl.ds(pl.multiple_of(t * LANES, LANES), LANES)]

                def cut(wide):
                    return [wide[:, i * LANES : (i + 1) * LANES] for i in range(group)]

                row = [edge(before)] + cut(source[s, :, span]) + [edge(after)]
                below, above = cut(source[s - 1, :, span]), cut(source[s + 1, :, span])
                rows = [cut(terms[w - 1, pl.ds(k, 1), span]) for k in range(7)]
                if not half_step:
                    older = cut(previous[previous_at(w), :, span])
                results = []
                for i in range(group):
                    left, here, right = row[i : i + 3]
                    total = rows[0][i] * here
                    total += rows[1][i] * below[i]
                    total += rows[2][i] * above[i]
                    total += rows[3][i] * pltpu.roll(jnp.where(first, right, here), LANES - 1, 1)
                    total += rows[4][i] * pltpu.roll(jnp.where(last, left, here), 1, 1)
                    total += rows[5][i] * pltpu.roll(jnp.where(head, right, here), LANES - NZ, 1)
                    total += rows[6][i] * pltpu.roll(jnp.where(tail, left, here), NZ, 1)
                    results.append(0.5 * total if half_step else total - older[i])
                result = jnp.concatenate(results, axis=1)
                if target is out:
                    half = lax.div(t0, per_half)
                    inner = pl.multiple_of((t0 - half * per_half) * LANES, LANES)
                    out[p * halves + half, :, pl.ds(inner, group * LANES)] = result
                else:
                    target[p, :, span] = result
                return carry

            return lax.fori_loop(0, tiles // group, group_body, carry, unroll=True)

        lax.fori_loop(0, count, plane_body, 0)

    def target_planes(target):
        return planes if target is out else target.shape[0]

    sweep(y0, lambda w: w, None, None, y1, 1, True)
    sweep(y1, lambda w: w - 1, y0, lambda w: w, y2, 2, False)
    sweep(y2, lambda w: w - 2, y1, lambda w: w - 1, y3, 3, False)
    sweep(y3, lambda w: w - 3, y2, lambda w: w - 2, out, 4, False)


def first_filter_kernel(planes, halves, scales, low, own, high, out, terms, *scratch):
    *fields, window = scratch
    terms_kernel(planes, scales, low, own, high, terms, window)
    filter_kernel(planes, halves, low, own, high, terms, out, *fields)


def filtered(low, own, high, blocks, terms=None, scales=None):
    planes, cells = own.shape[1:]
    halves = blocks // planes
    width = cells // halves
    steps = (3 * planes, 3 * planes - 2, 3 * planes - 4, 3 * planes - 6)
    vmem = pl.BlockSpec(memory_space=pltpu.VMEM)
    part = jax.ShapeDtypeStruct((blocks, CHUNK, width), jnp.float32)
    scratch = [pltpu.VMEM((count, CHUNK, cells), jnp.float32) for count in steps]
    options = dict(
        compiler_params=pltpu.CompilerParams(vmem_limit_bytes=32 * 2**20),
        cost_estimate=pl.CostEstimate(
            flops=14 * 7 * planes * CHUNK * cells,
            bytes_accessed=4 * 44 * CHUNK * cells,
            transcendentals=0,
        ),
    )
    if scales is None:
        return pl.pallas_call(
            functools.partial(filter_kernel, planes, halves),
            out_shape=part,
            in_specs=[vmem] * 4,
            out_specs=vmem,
            scratch_shapes=scratch,
            name="chebyshev",
            **options,
        )(low, own, high, terms)
    return pl.pallas_call(
        functools.partial(first_filter_kernel, planes, halves),
        out_shape=[part, jax.ShapeDtypeStruct((3 * planes - 2, 8, cells), jnp.float32)],
        in_specs=[pl.BlockSpec(memory_space=pltpu.SMEM)] + [vmem] * 3,
        out_specs=[vmem] * 2,
        scratch_shapes=scratch + [pltpu.VMEM((24, cells), jnp.float32)],
        name="first_chebyshev",
        **options,
    )(scales, low, own, high)


def rows_in_order(chunks):
    blocks = chunks[0].shape[0]
    return jnp.concatenate([c[b] for b in range(blocks) for c in chunks], axis=0)


def gram_kernel(*refs):
    *chunks, out = refs
    field = rows_in_order(chunks)
    update = lax.dot_general(
        field, field, (((1,), (1,)), ((), ())), precision=HIGHEST,
        preferred_element_type=jnp.float32,
    ).reshape(out.shape)

    @pl.when(pl.program_id(0) == 0)
    def _():
        out[...] = update

    @pl.when(pl.program_id(0) > 0)
    def _():
        out[...] += update


def partial_gram(chunks, pieces):
    blocks, rows, width = chunks[0].shape
    rank = blocks * rows * len(chunks)
    shape = (pieces, rank // pieces, rank)
    return pl.pallas_call(
        gram_kernel,
        grid=(width // BLOCK,),
        out_shape=jax.ShapeDtypeStruct(shape, jnp.float32),
        in_specs=[pl.BlockSpec((blocks, rows, BLOCK), lambda i: (0, 0, i))] * len(chunks),
        out_specs=pl.BlockSpec(shape, lambda i: (0, 0, 0)),
        compiler_params=pltpu.CompilerParams(vmem_limit_bytes=32 * 2**20),
        name="partial_gram",
    )(*chunks)


def product_kernel(inverse, *refs):
    *chunks, out = refs
    result = jnp.dot(
        inverse[...], rows_in_order(chunks), precision=HIGHEST,
        preferred_element_type=jnp.float32,
    )
    out[...] = result.reshape(out.shape)


def product(inverse, chunks):
    blocks, rows, width = chunks[0].shape
    rank = inverse.shape[0]
    return pl.pallas_call(
        product_kernel,
        grid=(width // BLOCK,),
        out_shape=jax.ShapeDtypeStruct((blocks, rank // blocks, width), jnp.float32),
        in_specs=[pl.BlockSpec((rank, rank), lambda i: (0, 0))]
        + [pl.BlockSpec((blocks, rows, BLOCK), lambda i: (0, 0, i))] * len(chunks),
        out_specs=pl.BlockSpec((blocks, rank // blocks, BLOCK), lambda i: (0, 0, i)),
        compiler_params=pltpu.CompilerParams(vmem_limit_bytes=32 * 2**20),
        name="product",
    )(inverse, *chunks)


def assemble_kernel(planes, source, out):
    for m in range(0, out.shape[0], 8):
        for p in range(planes):
            out[m : m + 8, p, :] = source[p, 0, m : m + 8, :]


def assembled(pieces):
    planes, halves, rows, width = pieces.shape
    return pl.pallas_call(
        functools.partial(assemble_kernel, planes),
        grid=(halves,),
        out_shape=jax.ShapeDtypeStruct((rows, planes, halves * width), jnp.float32),
        in_specs=[pl.BlockSpec((planes, 1, rows, width), lambda i: (0, i, 0, 0))],
        out_specs=pl.BlockSpec((rows, planes, width), lambda i: (0, 0, i)),
        compiler_params=pltpu.CompilerParams(vmem_limit_bytes=32 * 2**20),
        name="assemble",
    )(pieces)


def inverse_factor_kernel(scale, gram, out, work):
    rank = gram.shape[0]
    work[...] = gram[...] * scale
    lane = lax.broadcasted_iota(jnp.int32, (8, LANES), 1)
    sub = lax.broadcasted_iota(jnp.int32, (8, LANES), 0)
    wide = (8, LANES)
    parts = rank // LANES
    count = PANEL // 8
    for k0 in range(0, rank, PANEL):
        groups = [
            [work[k0 + 8 * g : k0 + 8 * g + 8, LANES * h : LANES * h + LANES] for h in range(parts)]
            for g in range(count)
        ]
        pivots = []
        for at in range(count):
            first = k0 + 8 * at
            home, start = first // LANES, first % LANES
            spread = {
                g: [
                    jnp.broadcast_to(groups[g][home][:, start + j : start + j + 1], wide)
                    for j in range(8)
                ]
                for g in range(at, count)
            }
            kept_pivots = jnp.ones(wide, jnp.float32)
            for j in range(8):
                pivot = jnp.broadcast_to(spread[at][j][j : j + 1, :], wide)
                inverse = 1.0 / pivot
                kept_pivots = jnp.where(sub == j, pivot, kept_pivots)
                here = lane == start + j
                rows = [jnp.broadcast_to(v[j : j + 1, :], wide) for v in groups[at]]
                rows[home] = jnp.where(here, 1.0, rows[home])
                later = {
                    i: jnp.broadcast_to(spread[at][i][j : j + 1, :], wide) for i in range(j + 1, 8)
                }
                for g in range(at, count):
                    factor = spread[g][j] * inverse
                    kept = list(groups[g])
                    if g == at:
                        factor = jnp.where(sub > j, factor, 0.0)
                        kept[home] = jnp.where(
                            here & (sub >= j), jnp.where(sub == j, 1.0, 0.0), kept[home]
                        )
                    else:
                        kept[home] = jnp.where(here, 0.0, kept[home])
                    groups[g] = [v - factor * r for v, r in zip(kept, rows)]
                    for i in range(j + 1, 8):
                        spread[g][i] = spread[g][i] - factor * later[i]
            pivots.append(1.0 / jnp.sqrt(kept_pivots))
        panel = jnp.concatenate(
            [
                jnp.concatenate([v * p for v in group], axis=1)
                for group, p in zip(groups, pivots)
            ],
            axis=0,
        )
        done = k0 + PANEL
        columns = lax.broadcasted_iota(jnp.int32, (PANEL, rank), 1)
        rows = k0 + lax.broadcasted_iota(jnp.int32, (PANEL, rank), 0)
        behind = columns <= rows
        out[k0:done, :] = jnp.where(behind, panel, 0.0)
        panel = jnp.where(behind | (columns >= done), panel, 0.0)
        if done < rank:
            update = lax.dot_general(
                panel, panel, (((0,), (0,)), ((), ())), precision=HIGHEST,
                preferred_element_type=jnp.float32,
            )
            inside = (columns[:1] >= k0) & (columns[:1] < done)
            work[done:, :] = jnp.where(inside, 0.0, work[done:, :]) - update[done:, :]


def inverse_factor(gram, scale):
    rank = gram.shape[0]
    return pl.pallas_call(
        functools.partial(inverse_factor_kernel, scale),
        out_shape=jax.ShapeDtypeStruct((rank, rank), jnp.float32),
        in_specs=[pl.BlockSpec(memory_space=pltpu.VMEM)],
        out_specs=pl.BlockSpec(memory_space=pltpu.VMEM),
        scratch_shapes=[pltpu.VMEM((rank, rank), jnp.float32)],
        name="inverse_factor",
    )(gram)


def local(start_vectors, phase_labels, phase_conductivity):
    upper_bound = 12.0 * jnp.max(phase_conductivity)
    lower_bound = upper_bound / 10.0
    centre = (upper_bound + lower_bound) / 2.0
    radius = (upper_bound - lower_bound) / 2.0
    per_device, planes, plane_cells = start_vectors.shape
    blocks, slabs = lax.axis_size("block"), lax.axis_size("space")
    assert planes == DEGREE and blocks % planes == 0
    halves = blocks // planes
    width = plane_cells // halves
    cells = planes * slabs * plane_cells
    rank = per_device * blocks
    up, back = neighbours("space")
    chunks = per_device // CHUNK

    scales = jnp.stack([2.0 / radius, centre])
    received = []
    for c in range(chunks):
        if c == 0:
            own = first_chunk(start_vectors, phase_labels, phase_conductivity)
        else:
            own = start_vectors[c * CHUNK : (c + 1) * CHUNK]
        low = lax.ppermute(own, "space", up)
        high = lax.ppermute(own, "space", back)
        if c == 0:
            part, terms = filtered(low, own, high, blocks, scales=scales)
        else:
            part = filtered(low, own, high, blocks, terms=terms)
        received.append(lax.all_to_all(part, "block", 0, 0, tiled=True))
    devices = blocks * slabs
    pieces = partial_gram(received, devices)
    summed = jnp.sum(lax.all_to_all(pieces, ("space", "block"), 0, 0, tiled=True), axis=0)
    gram = lax.all_to_all(
        jnp.broadcast_to(summed[None], pieces.shape), ("space", "block"), 0, 0, tiled=True
    ).reshape(rank, rank)
    inverse = inverse_factor(gram, 1.0 / cells)
    result = product(inverse, received)
    sent = lax.all_to_all(result, "block", 0, 0, tiled=True)
    return assembled(sent.reshape(planes, halves, per_device, width))


def solution(mesh):
    return jax.shard_map(
        local,
        mesh=mesh,
        in_specs=(P("block", "space", None), P("space", None), P()),
        out_specs=P("block", "space", None),
        check_vma=False,
    )
```

```python
import functools
import math

import jax
import jax.numpy as jnp
from jax import lax
from jax.experimental import pallas as pl
from jax.experimental.pallas import tpu as pltpu
from jax.sharding import PartitionSpec as P

NZ = 96
DEGREE = 4
LANES = 128
CHUNK = 8
PANEL = 64
BLOCK = 9 * LANES
HIGHEST = lax.Precision.HIGHEST


def neighbours(axis):
    count = lax.axis_size(axis)
    up = [(i, i + 1) for i in range(count - 1)]
    return up, [(b, a) for a, b in up]


def first_chunk_kernel(table, labels, vectors, out):
    out[0:CHUNK] = vectors[...]
    phase = labels[...]
    out[CHUNK] = jnp.where(phase == 0, table[0], jnp.where(phase == 1, table[1], table[2]))


def first_chunk(vectors, labels, table):
    planes, cells = labels.shape
    return pl.pallas_call(
        first_chunk_kernel,
        grid=(1,),
        out_shape=jax.ShapeDtypeStruct((CHUNK + 1, planes, cells), jnp.float32),
        in_specs=[
            pl.BlockSpec(memory_space=pltpu.SMEM),
            pl.BlockSpec((planes, cells), lambda i: (0, 0)),
            pl.BlockSpec((CHUNK, planes, cells), lambda i: (0, 0, 0)),
        ],
        out_specs=pl.BlockSpec((CHUNK + 1, planes, cells), lambda i: (0, 0, 0)),
        name="first_chunk",
    )(table, labels, vectors)


def face(left_k, right_k):
    filled = jnp.where(right_k > 0, right_k, left_k)
    return 2.0 * left_k * filled / (left_k + filled)


def terms_kernel(planes, scales, raw, out, window):
    scale, shift = scales[0], scales[1]
    count = out.shape[0]
    window[...] = jnp.zeros_like(window)
    for k in range(3):
        window[k * planes : (k + 1) * planes, :] = raw[k, CHUNK]
    cells = window.shape[1]
    span = 3 * LANES * NZ // math.gcd(3 * LANES, NZ)
    assert cells % span == 0
    z = lax.rem(lax.broadcasted_iota(jnp.int32, (8, span), 1), NZ)

    def body(g, carry):
        lanes = pl.ds(pl.multiple_of(g * span, span), span)
        left = pl.ds(pl.multiple_of(jnp.maximum(g * span - LANES, 0), LANES), LANES)
        right = pl.ds(
            pl.multiple_of(jnp.minimum(g * span + span, cells - LANES), LANES), LANES
        )
        for base in range(0, count, 8):
            rows = pl.ds(base + 1, 8)
            kappa = window[rows, lanes]
            inside = kappa > 0
            safe = jnp.where(inside, kappa, 1.0)
            before = jnp.where(g == 0, 0.0, window[rows, left])
            after = jnp.where(g * span + span == cells, 0.0, window[rows, right])
            wide = jnp.concatenate([before, kappa, after], axis=1)
            total = wide.shape[1]

            def moved(offset):
                return pltpu.roll(wide, (-offset) % total, 1)[:, LANES : LANES + span]

            around = [
                window[pl.ds(base, 8), lanes],
                window[pl.ds(base + 2, 8), lanes],
                jnp.where(z < NZ - 1, moved(1), 0.0),
                jnp.where(z > 0, moved(-1), 0.0),
                moved(NZ),
                moved(-NZ),
            ]
            faces = [face(safe, k) for k in around]
            diagonal = functools.reduce(jnp.add, faces) - shift
            values = [jnp.where(inside, diagonal * scale, 0.0)]
            for f, k in zip(faces, around):
                values.append(jnp.where(inside & (k > 0), -scale * f, 0.0))
            kept = min(8, count - base)
            for k, value in enumerate(values):
                out[base : base + kept, k, lanes] = value[:kept]
        return carry

    lax.fori_loop(0, cells // span, body, 0)


def start_reading(sources, raw, sems):
    copies = [
        pltpu.make_async_copy(source, raw.at[k], sems.at[k]) for k, source in enumerate(sources)
    ]
    for copy in copies:
        copy.start()
    return copies


def filter_kernel(planes, halves, raw, terms, target_array, out, sems, y0, y1, y2, y3):
    for k in range(3):
        for p in range(planes):
            y0[k * planes + p] = raw[k, 0:CHUNK, p, :]
    cells = y0.shape[-1]
    tiles = cells // LANES
    per_half = tiles // halves
    group = per_half
    lane = lax.broadcasted_iota(jnp.int32, (CHUNK, LANES), 1)
    last, first = lane == LANES - 1, lane == 0
    head, tail = lane < NZ, lane >= LANES - NZ

    def sweep(source, source_at, previous, previous_at, target, at, half_step):
        count = target_planes(target)

        def plane_body(p, carry):
            w = p + at

            def group_body(g, carry):
                t0 = g * group
                s = source_at(w)
                span = pl.ds(pl.multiple_of(t0 * LANES, LANES), group * LANES)
                before = jnp.where(t0 == 0, tiles - 1, t0 - 1)
                after = jnp.where(t0 + group == tiles, 0, t0 + group)

                def edge(t):
                    return source[s, :, pl.ds(pl.multiple_of(t * LANES, LANES), LANES)]

                def cut(wide):
                    return [wide[:, i * LANES : (i + 1) * LANES] for i in range(group)]

                row = [edge(before)] + cut(source[s, :, span]) + [edge(after)]
                below, above = cut(source[s - 1, :, span]), cut(source[s + 1, :, span])
                rows = [cut(terms[w - 1, pl.ds(k, 1), span]) for k in range(7)]
                if not half_step:
                    older = cut(previous[previous_at(w), :, span])
                results = []
                for i in range(group):
                    left, here, right = row[i : i + 3]
                    total = rows[0][i] * here
                    total += rows[1][i] * below[i]
                    total += rows[2][i] * above[i]
                    total += rows[3][i] * pltpu.roll(jnp.where(first, right, here), LANES - 1, 1)
                    total += rows[4][i] * pltpu.roll(jnp.where(last, left, here), 1, 1)
                    total += rows[5][i] * pltpu.roll(jnp.where(head, right, here), LANES - NZ, 1)
                    total += rows[6][i] * pltpu.roll(jnp.where(tail, left, here), NZ, 1)
                    results.append(0.5 * total if half_step else total - older[i])
                result = jnp.concatenate(results, axis=1)
                if target is out:
                    half = lax.div(t0, per_half)
                    inner = pl.multiple_of((t0 - half * per_half) * LANES, LANES)
                    out[p * halves + half, :, pl.ds(inner, group * LANES)] = result
                else:
                    target[p, :, span] = result
                return carry

            lax.fori_loop(0, tiles // group, group_body, 0, unroll=True)
            if target is out:
                leaving(p).start()
            return carry

        lax.fori_loop(0, count, plane_body, 0)

    def target_planes(target):
        return planes if target is out else target.shape[0]

    def leaving(p):
        rows = pl.ds(p * halves, halves)
        return pltpu.make_async_copy(out.at[rows], target_array.at[rows], sems.at[p])

    sweep(y0, lambda w: w, None, None, y1, 1, True)
    sweep(y1, lambda w: w - 1, y0, lambda w: w, y2, 2, False)
    sweep(y2, lambda w: w - 2, y1, lambda w: w - 1, y3, 3, False)
    sweep(y3, lambda w: w - 3, y2, lambda w: w - 2, out, 4, False)
    for p in range(planes):
        leaving(p).wait()


def next_filter_kernel(
    planes, halves, low, own, high, stored, target, raw, sems, out, y0, y1, y2, y3, terms
):
    copies = start_reading((low, own, high), raw, sems)
    last = pltpu.make_async_copy(stored, terms, sems.at[3 + planes])
    last.start()
    for copy in copies:
        copy.wait()
    last.wait()
    filter_kernel(
        planes, halves, raw, terms, target, out, sems.at[pl.ds(3, planes)], y0, y1, y2, y3
    )


def first_filter_kernel(
    planes, halves, scales, low, own, high, target, stored, raw, sems, out, y0, y1, y2, y3, terms, window
):
    for copy in start_reading((low, own, high), raw, sems):
        copy.wait()
    terms_kernel(planes, scales, raw, terms, window)
    last = pltpu.make_async_copy(terms, stored, sems.at[3 + planes])
    last.start()
    filter_kernel(
        planes, halves, raw, terms, target, out, sems.at[pl.ds(3, planes)], y0, y1, y2, y3
    )
    last.wait()


def filtered(low, own, high, blocks, terms=None, scales=None):
    rows, planes, cells = own.shape
    halves = blocks // planes
    width = cells // halves
    steps = (3 * planes, 3 * planes - 2, 3 * planes - 4, 3 * planes - 6)
    hbm = pl.BlockSpec(memory_space=pltpu.HBM)
    part = jax.ShapeDtypeStruct((blocks, CHUNK, width), jnp.float32)
    scratch = [
        pltpu.VMEM((3, rows, planes, cells), jnp.float32),
        pltpu.SemaphoreType.DMA((4 + planes,)),
        pltpu.VMEM(part.shape, jnp.float32),
    ]
    scratch += [pltpu.VMEM((count, CHUNK, cells), jnp.float32) for count in steps]
    factors = jax.ShapeDtypeStruct((3 * planes - 2, 8, cells), jnp.float32)
    scratch.append(pltpu.VMEM(factors.shape, jnp.float32))
    options = dict(
        compiler_params=pltpu.CompilerParams(vmem_limit_bytes=60 * 2**20),
        cost_estimate=pl.CostEstimate(
            flops=14 * 7 * planes * CHUNK * cells,
            bytes_accessed=4 * 44 * CHUNK * cells,
            transcendentals=0,
        ),
    )
    if scales is None:
        return pl.pallas_call(
            functools.partial(next_filter_kernel, planes, halves),
            out_shape=part,
            in_specs=[hbm] * 4,
            out_specs=hbm,
            scratch_shapes=scratch,
            name="chebyshev",
            **options,
        )(low, own, high, terms)
    return pl.pallas_call(
        functools.partial(first_filter_kernel, planes, halves),
        out_shape=[part, factors],
        in_specs=[pl.BlockSpec(memory_space=pltpu.SMEM)] + [hbm] * 3,
        out_specs=[hbm] * 2,
        scratch_shapes=scratch + [pltpu.VMEM((24, cells), jnp.float32)],
        name="first_chebyshev",
        **options,
    )(scales, low, own, high)


def rows_in_order(chunks):
    blocks = chunks[0].shape[0]
    return jnp.concatenate([c[b] for b in range(blocks) for c in chunks], axis=0)


def gram_kernel(*refs):
    *chunks, out = refs
    field = rows_in_order(chunks)
    update = lax.dot_general(
        field, field, (((1,), (1,)), ((), ())), precision=HIGHEST,
        preferred_element_type=jnp.float32,
    ).reshape(out.shape)

    @pl.when(pl.program_id(0) == 0)
    def _():
        out[...] = update

    @pl.when(pl.program_id(0) > 0)
    def _():
        out[...] += update


def partial_gram(chunks, pieces):
    blocks, rows, width = chunks[0].shape
    rank = blocks * rows * len(chunks)
    shape = (pieces, rank // pieces, rank)
    return pl.pallas_call(
        gram_kernel,
        grid=(width // BLOCK,),
        out_shape=jax.ShapeDtypeStruct(shape, jnp.float32),
        in_specs=[pl.BlockSpec((blocks, rows, BLOCK), lambda i: (0, 0, i))] * len(chunks),
        out_specs=pl.BlockSpec(shape, lambda i: (0, 0, 0)),
        compiler_params=pltpu.CompilerParams(vmem_limit_bytes=60 * 2**20),
        name="partial_gram",
    )(*chunks)


def halved(value):
    high = value.astype(jnp.bfloat16)
    return high, (value - high.astype(jnp.float32)).astype(jnp.bfloat16)


def dot(left, right):
    return jnp.dot(left, right, preferred_element_type=jnp.float32)


def product_kernel(inverse, *refs):
    *chunks, out = refs
    (a, b), (x, y) = halved(inverse[...]), halved(rows_in_order(chunks))
    out[...] = (dot(a, x) + (dot(a, y) + dot(b, x))).reshape(out.shape)


def product(inverse, chunks):
    blocks, rows, width = chunks[0].shape
    rank = inverse.shape[0]
    return pl.pallas_call(
        product_kernel,
        grid=(width // BLOCK,),
        out_shape=jax.ShapeDtypeStruct((blocks, rank // blocks, width), jnp.float32),
        in_specs=[pl.BlockSpec((rank, rank), lambda i: (0, 0))]
        + [pl.BlockSpec((blocks, rows, BLOCK), lambda i: (0, 0, i))] * len(chunks),
        out_specs=pl.BlockSpec((blocks, rank // blocks, BLOCK), lambda i: (0, 0, i)),
        compiler_params=pltpu.CompilerParams(vmem_limit_bytes=60 * 2**20),
        name="product",
    )(inverse, *chunks)


def assemble_kernel(planes, source, out):
    for m in range(0, out.shape[0], 8):
        for p in range(planes):
            out[m : m + 8, p, :] = source[p, 0, m : m + 8, :]


def assembled(pieces):
    planes, halves, rows, width = pieces.shape
    return pl.pallas_call(
        functools.partial(assemble_kernel, planes),
        grid=(halves,),
        out_shape=jax.ShapeDtypeStruct((rows, planes, halves * width), jnp.float32),
        in_specs=[pl.BlockSpec((planes, 1, rows, width), lambda i: (0, i, 0, 0))],
        out_specs=pl.BlockSpec((rows, planes, width), lambda i: (0, 0, i)),
        compiler_params=pltpu.CompilerParams(vmem_limit_bytes=60 * 2**20),
        name="assemble",
    )(pieces)


def inverse_factor_kernel(scale, gram, out, work):
    rank = gram.shape[0]
    work[...] = gram[...] * scale
    lane = lax.broadcasted_iota(jnp.int32, (8, LANES), 1)
    sub = lax.broadcasted_iota(jnp.int32, (8, LANES), 0)
    wide = (8, LANES)
    parts = rank // LANES
    count = PANEL // 8
    for k0 in range(0, rank, PANEL):
        groups = [
            [work[k0 + 8 * g : k0 + 8 * g + 8, LANES * h : LANES * h + LANES] for h in range(parts)]
            for g in range(count)
        ]
        pivots = []
        for at in range(count):
            first = k0 + 8 * at
            home, start = first // LANES, first % LANES
            spread = {
                g: [
                    jnp.broadcast_to(groups[g][home][:, start + j : start + j + 1], wide)
                    for j in range(8)
                ]
                for g in range(at, count)
            }
            kept_pivots = jnp.ones(wide, jnp.float32)
            for j in range(8):
                pivot = jnp.broadcast_to(spread[at][j][j : j + 1, :], wide)
                inverse = 1.0 / pivot
                kept_pivots = jnp.where(sub == j, pivot, kept_pivots)
                here = lane == start + j
                rows = [jnp.broadcast_to(v[j : j + 1, :], wide) for v in groups[at]]
                rows[home] = jnp.where(here, 1.0, rows[home])
                later = {
                    i: jnp.broadcast_to(spread[at][i][j : j + 1, :], wide) for i in range(j + 1, 8)
                }
                for g in range(at, count):
                    factor = spread[g][j] * inverse
                    kept = list(groups[g])
                    if g == at:
                        factor = jnp.where(sub > j, factor, 0.0)
                        kept[home] = jnp.where(
                            here & (sub >= j), jnp.where(sub == j, 1.0, 0.0), kept[home]
                        )
                    else:
                        kept[home] = jnp.where(here, 0.0, kept[home])
                    groups[g] = [v - factor * r for v, r in zip(kept, rows)]
                    for i in range(j + 1, 8):
                        spread[g][i] = spread[g][i] - factor * later[i]
            pivots.append(1.0 / jnp.sqrt(kept_pivots))
        panel = jnp.concatenate(
            [
                jnp.concatenate([v * p for v in group], axis=1)
                for group, p in zip(groups, pivots)
            ],
            axis=0,
        )
        done = k0 + PANEL
        columns = lax.broadcasted_iota(jnp.int32, (PANEL, rank), 1)
        rows = k0 + lax.broadcasted_iota(jnp.int32, (PANEL, rank), 0)
        behind = columns <= rows
        out[k0:done, :] = jnp.where(behind, panel, 0.0)
        panel = jnp.where(behind | (columns >= done), panel, 0.0)
        if done < rank:
            update = lax.dot_general(
                panel, panel, (((0,), (0,)), ((), ())), precision=HIGHEST,
                preferred_element_type=jnp.float32,
            )
            inside = (columns[:1] >= k0) & (columns[:1] < done)
            work[done:, :] = jnp.where(inside, 0.0, work[done:, :]) - update[done:, :]


def inverse_factor(gram, scale):
    rank = gram.shape[0]
    return pl.pallas_call(
        functools.partial(inverse_factor_kernel, scale),
        out_shape=jax.ShapeDtypeStruct((rank, rank), jnp.float32),
        in_specs=[pl.BlockSpec(memory_space=pltpu.VMEM)],
        out_specs=pl.BlockSpec(memory_space=pltpu.VMEM),
        scratch_shapes=[pltpu.VMEM((rank, rank), jnp.float32)],
        name="inverse_factor",
    )(gram)


def local(start_vectors, phase_labels, phase_conductivity):
    upper_bound = 12.0 * jnp.max(phase_conductivity)
    lower_bound = upper_bound / 10.0
    centre = (upper_bound + lower_bound) / 2.0
    radius = (upper_bound - lower_bound) / 2.0
    per_device, planes, plane_cells = start_vectors.shape
    blocks, slabs = lax.axis_size("block"), lax.axis_size("space")
    assert planes == DEGREE and blocks % planes == 0
    halves = blocks // planes
    width = plane_cells // halves
    cells = planes * slabs * plane_cells
    rank = per_device * blocks
    up, back = neighbours("space")
    chunks = per_device // CHUNK

    scales = jnp.stack([2.0 / radius, centre])
    received = []
    for c in range(chunks):
        if c == 0:
            own = first_chunk(start_vectors, phase_labels, phase_conductivity)
        else:
            own = start_vectors[c * CHUNK : (c + 1) * CHUNK]
        low = lax.ppermute(own, "space", up)
        high = lax.ppermute(own, "space", back)
        if c == 0:
            part, terms = filtered(low, own, high, blocks, scales=scales)
        else:
            part = filtered(low, own, high, blocks, terms=terms)
        received.append(lax.all_to_all(part, "block", 0, 0, tiled=True))
    devices = blocks * slabs
    pieces = partial_gram(received, devices)
    summed = jnp.sum(lax.all_to_all(pieces, ("space", "block"), 0, 0, tiled=True), axis=0)
    gram = lax.all_to_all(
        jnp.broadcast_to(summed[None], pieces.shape), ("space", "block"), 0, 0, tiled=True
    ).reshape(rank, rank)
    inverse = inverse_factor(gram, 1.0 / cells)
    result = product(inverse, received)
    sent = lax.all_to_all(result, "block", 0, 0, tiled=True)
    return assembled(sent.reshape(planes, halves, per_device, width))


def solution(mesh):
    return jax.shard_map(
        local,
        mesh=mesh,
        in_specs=(P("block", "space", None), P("space", None), P()),
        out_specs=P("block", "space", None),
        check_vma=False,
    )
```

```python
import functools
import math

import jax
import jax.numpy as jnp
from jax import lax
from jax.experimental import pallas as pl
from jax.experimental.pallas import tpu as pltpu
from jax.sharding import PartitionSpec as P

NZ = 96
DEGREE = 4
LANES = 128
CHUNK = 8
PANEL = 64
BLOCK = 18 * LANES
HIGHEST = lax.Precision.HIGHEST


def neighbours(axis):
    count = lax.axis_size(axis)
    up = [(i, i + 1) for i in range(count - 1)]
    return up, [(b, a) for a, b in up]


def first_chunk_kernel(table, labels, vectors, out):
    out[0:CHUNK] = vectors[...]
    phase = labels[...]
    out[CHUNK] = jnp.where(phase == 0, table[0], jnp.where(phase == 1, table[1], table[2]))


def first_chunk(vectors, labels, table):
    planes, cells = labels.shape
    return pl.pallas_call(
        first_chunk_kernel,
        grid=(1,),
        out_shape=jax.ShapeDtypeStruct((CHUNK + 1, planes, cells), jnp.float32),
        in_specs=[
            pl.BlockSpec(memory_space=pltpu.SMEM),
            pl.BlockSpec((planes, cells), lambda i: (0, 0)),
            pl.BlockSpec((CHUNK, planes, cells), lambda i: (0, 0, 0)),
        ],
        out_specs=pl.BlockSpec((CHUNK + 1, planes, cells), lambda i: (0, 0, 0)),
        name="first_chunk",
    )(table, labels, vectors)


def face(left_k, right_k):
    filled = jnp.where(right_k > 0, right_k, left_k)
    return 2.0 * left_k * filled / (left_k + filled)


def terms_kernel(planes, scales, raw, out, window):
    scale, shift = scales[0], scales[1]
    count = out.shape[0]
    window[...] = jnp.zeros_like(window)
    for k in range(3):
        window[k * planes : (k + 1) * planes, :] = raw[k, CHUNK]
    cells = window.shape[1]
    span = 3 * LANES * NZ // math.gcd(3 * LANES, NZ)
    assert cells % span == 0
    z = lax.rem(lax.broadcasted_iota(jnp.int32, (8, span), 1), NZ)

    def body(g, carry):
        lanes = pl.ds(pl.multiple_of(g * span, span), span)
        left = pl.ds(pl.multiple_of(jnp.maximum(g * span - LANES, 0), LANES), LANES)
        right = pl.ds(
            pl.multiple_of(jnp.minimum(g * span + span, cells - LANES), LANES), LANES
        )
        for base in range(0, count, 8):
            rows = pl.ds(base + 1, 8)
            kappa = window[rows, lanes]
            inside = kappa > 0
            safe = jnp.where(inside, kappa, 1.0)
            before = jnp.where(g == 0, 0.0, window[rows, left])
            after = jnp.where(g * span + span == cells, 0.0, window[rows, right])
            wide = jnp.concatenate([before, kappa, after], axis=1)
            total = wide.shape[1]

            def moved(offset):
                return pltpu.roll(wide, (-offset) % total, 1)[:, LANES : LANES + span]

            around = [
                window[pl.ds(base, 8), lanes],
                window[pl.ds(base + 2, 8), lanes],
                jnp.where(z < NZ - 1, moved(1), 0.0),
                jnp.where(z > 0, moved(-1), 0.0),
                moved(NZ),
                moved(-NZ),
            ]
            faces = [face(safe, k) for k in around]
            diagonal = functools.reduce(jnp.add, faces) - shift
            values = [jnp.where(inside, diagonal * scale, 0.0)]
            for f, k in zip(faces, around):
                values.append(jnp.where(inside & (k > 0), -scale * f, 0.0))
            kept = min(8, count - base)
            for k, value in enumerate(values):
                out[base : base + kept, k, lanes] = value[:kept]
        return carry

    lax.fori_loop(0, cells // span, body, 0)


def start_reading(sources, raw, sems):
    copies = [
        pltpu.make_async_copy(source, raw.at[k], sems.at[k]) for k, source in enumerate(sources)
    ]
    for copy in copies:
        copy.start()
    return copies


def filter_kernel(planes, halves, arriving, raw, terms, target_array, out, sems, y0, y1, y2, y3):
    for k in range(3):
        if k < len(arriving):
            arriving[k].wait()
        for p in range(planes):
            y0[k * planes + p] = raw[k, 0:CHUNK, p, :]
    for copy in arriving[3:]:
        copy.wait()
    cells = y0.shape[-1]
    tiles = cells // LANES
    per_half = tiles // halves
    lane = lax.broadcasted_iota(jnp.int32, (CHUNK, LANES), 1)
    last, first = lane == LANES - 1, lane == 0
    head, tail = lane < NZ, lane >= LANES - NZ

    def sweep(source, source_at, previous, previous_at, target, at, half_step):
        count = target_planes(target)

        def plane_body(p, carry):
            w = p + at

            s = source_at(w)

            def tile(array, plane, t):
                return array[plane, :, t * LANES : (t + 1) * LANES]

            row = [tile(source, s, tiles - 1), tile(source, s, 0)]
            for t in range(tiles):
                left, here = row
                right = tile(source, s, (t + 1) % tiles)
                row = [here, right]
                term = [terms[w - 1, k : k + 1, t * LANES : (t + 1) * LANES] for k in range(7)]
                total = term[0] * here
                total += term[1] * tile(source, s - 1, t)
                total += term[2] * tile(source, s + 1, t)
                total += term[3] * pltpu.roll(jnp.where(first, right, here), LANES - 1, 1)
                total += term[4] * pltpu.roll(jnp.where(last, left, here), 1, 1)
                total += term[5] * pltpu.roll(jnp.where(head, right, here), LANES - NZ, 1)
                total += term[6] * pltpu.roll(jnp.where(tail, left, here), NZ, 1)
                total = 0.5 * total if half_step else total - tile(previous, previous_at(w), t)
                if target is out:
                    inner = t % per_half * LANES
                    out[p * halves + t // per_half, :, inner : inner + LANES] = total
                else:
                    target[p, :, t * LANES : (t + 1) * LANES] = total
            if target is out:
                leaving(p).start()
            return carry

        lax.fori_loop(0, count, plane_body, 0)

    def target_planes(target):
        return planes if target is out else target.shape[0]

    def leaving(p):
        rows = pl.ds(p * halves, halves)
        return pltpu.make_async_copy(out.at[rows], target_array.at[rows], sems.at[p])

    sweep(y0, lambda w: w, None, None, y1, 1, True)
    sweep(y1, lambda w: w - 1, y0, lambda w: w, y2, 2, False)
    sweep(y2, lambda w: w - 2, y1, lambda w: w - 1, y3, 3, False)
    sweep(y3, lambda w: w - 3, y2, lambda w: w - 2, out, 4, False)
    for p in range(planes):
        leaving(p).wait()


def next_filter_kernel(
    planes, halves, low, own, high, stored, target, raw, sems, out, y0, y1, y2, y3, terms
):
    copies = start_reading((low, own, high), raw, sems)
    last = pltpu.make_async_copy(stored, terms, sems.at[3 + planes])
    last.start()
    filter_kernel(
        planes, halves, (*copies, last), raw, terms, target, out, sems.at[pl.ds(3, planes)], y0, y1, y2, y3
    )


def first_filter_kernel(
    planes, halves, scales, low, own, high, target, stored, raw, sems, out, y0, y1, y2, y3, terms, window
):
    for copy in start_reading((low, own, high), raw, sems):
        copy.wait()
    terms_kernel(planes, scales, raw, terms, window)
    last = pltpu.make_async_copy(terms, stored, sems.at[3 + planes])
    last.start()
    filter_kernel(
        planes, halves, (), raw, terms, target, out, sems.at[pl.ds(3, planes)], y0, y1, y2, y3
    )
    last.wait()


def filtered(low, own, high, blocks, terms=None, scales=None):
    rows, planes, cells = own.shape
    halves = blocks // planes
    width = cells // halves
    steps = (3 * planes, 3 * planes - 2, 3 * planes - 4, 3 * planes - 6)
    hbm = pl.BlockSpec(memory_space=pltpu.HBM)
    part = jax.ShapeDtypeStruct((blocks, CHUNK, width), jnp.float32)
    scratch = [
        pltpu.VMEM((3, rows, planes, cells), jnp.float32),
        pltpu.SemaphoreType.DMA((4 + planes,)),
        pltpu.VMEM(part.shape, jnp.float32),
    ]
    scratch += [pltpu.VMEM((count, CHUNK, cells), jnp.float32) for count in steps]
    factors = jax.ShapeDtypeStruct((3 * planes - 2, 8, cells), jnp.float32)
    scratch.append(pltpu.VMEM(factors.shape, jnp.float32))
    options = dict(
        compiler_params=pltpu.CompilerParams(vmem_limit_bytes=60 * 2**20),
        cost_estimate=pl.CostEstimate(
            flops=14 * 7 * planes * CHUNK * cells,
            bytes_accessed=4 * 44 * CHUNK * cells,
            transcendentals=0,
        ),
    )
    if scales is None:
        return pl.pallas_call(
            functools.partial(next_filter_kernel, planes, halves),
            out_shape=part,
            in_specs=[hbm] * 4,
            out_specs=hbm,
            scratch_shapes=scratch,
            name="chebyshev",
            **options,
        )(low, own, high, terms)
    return pl.pallas_call(
        functools.partial(first_filter_kernel, planes, halves),
        out_shape=[part, factors],
        in_specs=[pl.BlockSpec(memory_space=pltpu.SMEM)] + [hbm] * 3,
        out_specs=[hbm] * 2,
        scratch_shapes=scratch + [pltpu.VMEM((24, cells), jnp.float32)],
        name="first_chebyshev",
        **options,
    )(scales, low, own, high)


def rows_in_order(chunks):
    blocks = chunks[0].shape[0]
    return jnp.concatenate([c[b] for b in range(blocks) for c in chunks], axis=0)


def halved(value):
    high = value.astype(jnp.bfloat16)
    return high, (value - high.astype(jnp.float32)).astype(jnp.bfloat16)


def dot(left, right):
    return jnp.dot(left, right, preferred_element_type=jnp.float32)


def gram_kernel(*refs):
    *chunks, out, cross = refs
    step = pl.program_id(0)
    rank = cross.shape[0]
    high, low = halved(rows_in_order(chunks))

    def inner(left, right):
        return lax.dot_general(
            left, right, (((1,), (1,)), ((), ())), preferred_element_type=jnp.float32
        )

    square, mixed = inner(high, high).reshape(out.shape), inner(high, low)

    @pl.when(step == 0)
    def _():
        out[...] = square
        cross[...] = mixed

    @pl.when(step > 0)
    def _():
        out[...] += square
        cross[...] += mixed

    @pl.when(step == pl.num_programs(0) - 1)
    def _():
        both = cross[...] + jnp.transpose(cross[...])
        out[...] += both.reshape(out.shape)


def partial_gram(chunks, pieces):
    blocks, rows, width = chunks[0].shape
    rank = blocks * rows * len(chunks)
    shape = (pieces, rank // pieces, rank)
    return pl.pallas_call(
        gram_kernel,
        grid=(width // BLOCK,),
        out_shape=jax.ShapeDtypeStruct(shape, jnp.float32),
        in_specs=[pl.BlockSpec((blocks, rows, BLOCK), lambda i: (0, 0, i))] * len(chunks),
        out_specs=pl.BlockSpec(shape, lambda i: (0, 0, 0)),
        scratch_shapes=[pltpu.VMEM((rank, rank), jnp.float32)],
        compiler_params=pltpu.CompilerParams(vmem_limit_bytes=60 * 2**20),
        name="partial_gram",
    )(*chunks)


def product_kernel(inverse, *refs):
    *chunks, out = refs
    (a, b), (x, y) = halved(inverse[...]), halved(rows_in_order(chunks))
    out[...] = (dot(a, x) + (dot(a, y) + dot(b, x))).reshape(out.shape)


def product(inverse, chunks):
    blocks, rows, width = chunks[0].shape
    rank = inverse.shape[0]
    return pl.pallas_call(
        product_kernel,
        grid=(width // BLOCK,),
        out_shape=jax.ShapeDtypeStruct((blocks, rank // blocks, width), jnp.float32),
        in_specs=[pl.BlockSpec((rank, rank), lambda i: (0, 0))]
        + [pl.BlockSpec((blocks, rows, BLOCK), lambda i: (0, 0, i))] * len(chunks),
        out_specs=pl.BlockSpec((blocks, rank // blocks, BLOCK), lambda i: (0, 0, i)),
        compiler_params=pltpu.CompilerParams(vmem_limit_bytes=60 * 2**20),
        name="product",
    )(inverse, *chunks)


def assemble_kernel(planes, source, out):
    for m in range(0, out.shape[0], 8):
        for p in range(planes):
            out[m : m + 8, p, :] = source[p, 0, m : m + 8, :]


def assembled(pieces):
    planes, halves, rows, width = pieces.shape
    return pl.pallas_call(
        functools.partial(assemble_kernel, planes),
        grid=(halves,),
        out_shape=jax.ShapeDtypeStruct((rows, planes, halves * width), jnp.float32),
        in_specs=[pl.BlockSpec((planes, 1, rows, width), lambda i: (0, i, 0, 0))],
        out_specs=pl.BlockSpec((rows, planes, width), lambda i: (0, 0, i)),
        compiler_params=pltpu.CompilerParams(vmem_limit_bytes=32 * 2**20),
        name="assemble",
    )(pieces)


def inverse_factor_kernel(scale, gram, out, work):
    rank = gram.shape[0]
    work[...] = gram[...] * scale
    lane = lax.broadcasted_iota(jnp.int32, (8, LANES), 1)
    sub = lax.broadcasted_iota(jnp.int32, (8, LANES), 0)
    wide = (8, LANES)
    parts = rank // LANES
    count = PANEL // 8
    for k0 in range(0, rank, PANEL):
        groups = [
            [work[k0 + 8 * g : k0 + 8 * g + 8, LANES * h : LANES * h + LANES] for h in range(parts)]
            for g in range(count)
        ]
        pivots = []
        for at in range(count):
            first = k0 + 8 * at
            home, start = first // LANES, first % LANES
            spread = {
                g: [
                    jnp.broadcast_to(groups[g][home][:, start + j : start + j + 1], wide)
                    for j in range(8)
                ]
                for g in range(at, count)
            }
            kept_pivots = jnp.ones(wide, jnp.float32)
            for j in range(8):
                pivot = jnp.broadcast_to(spread[at][j][j : j + 1, :], wide)
                inverse = 1.0 / pivot
                kept_pivots = jnp.where(sub == j, pivot, kept_pivots)
                here = lane == start + j
                rows = [jnp.broadcast_to(v[j : j + 1, :], wide) for v in groups[at]]
                rows[home] = jnp.where(here, 1.0, rows[home])
                later = {
                    i: jnp.broadcast_to(spread[at][i][j : j + 1, :], wide) for i in range(j + 1, 8)
                }
                for g in range(at, count):
                    factor = spread[g][j] * inverse
                    kept = list(groups[g])
                    if g == at:
                        factor = jnp.where(sub > j, factor, 0.0)
                        kept[home] = jnp.where(
                            here & (sub >= j), jnp.where(sub == j, 1.0, 0.0), kept[home]
                        )
                    else:
                        kept[home] = jnp.where(here, 0.0, kept[home])
                    groups[g] = [v - factor * r for v, r in zip(kept, rows)]
                    for i in range(j + 1, 8):
                        spread[g][i] = spread[g][i] - factor * later[i]
            pivots.append(1.0 / jnp.sqrt(kept_pivots))
        panel = jnp.concatenate(
            [
                jnp.concatenate([v * p for v in group], axis=1)
                for group, p in zip(groups, pivots)
            ],
            axis=0,
        )
        done = k0 + PANEL
        columns = lax.broadcasted_iota(jnp.int32, (PANEL, rank), 1)
        rows = k0 + lax.broadcasted_iota(jnp.int32, (PANEL, rank), 0)
        behind = columns <= rows
        out[k0:done, :] = jnp.where(behind, panel, 0.0)
        panel = jnp.where(behind | (columns >= done), panel, 0.0)
        if done < rank:
            update = lax.dot_general(
                panel, panel, (((0,), (0,)), ((), ())), precision=HIGHEST,
                preferred_element_type=jnp.float32,
            )
            inside = (columns[:1] >= k0) & (columns[:1] < done)
            work[done:, :] = jnp.where(inside, 0.0, work[done:, :]) - update[done:, :]


def inverse_factor(gram, scale):
    rank = gram.shape[0]
    return pl.pallas_call(
        functools.partial(inverse_factor_kernel, scale),
        out_shape=jax.ShapeDtypeStruct((rank, rank), jnp.float32),
        in_specs=[pl.BlockSpec(memory_space=pltpu.VMEM)],
        out_specs=pl.BlockSpec(memory_space=pltpu.VMEM),
        scratch_shapes=[pltpu.VMEM((rank, rank), jnp.float32)],
        name="inverse_factor",
    )(gram)


def local(start_vectors, phase_labels, phase_conductivity):
    upper_bound = 12.0 * jnp.max(phase_conductivity)
    lower_bound = upper_bound / 10.0
    centre = (upper_bound + lower_bound) / 2.0
    radius = (upper_bound - lower_bound) / 2.0
    per_device, planes, plane_cells = start_vectors.shape
    blocks, slabs = lax.axis_size("block"), lax.axis_size("space")
    assert planes == DEGREE and blocks % planes == 0
    halves = blocks // planes
    width = plane_cells // halves
    cells = planes * slabs * plane_cells
    rank = per_device * blocks
    up, back = neighbours("space")
    chunks = per_device // CHUNK

    scales = jnp.stack([2.0 / radius, centre])
    received = []
    for c in range(chunks):
        if c == 0:
            own = first_chunk(start_vectors, phase_labels, phase_conductivity)
        else:
            own = start_vectors[c * CHUNK : (c + 1) * CHUNK]
        low = lax.ppermute(own, "space", up)
        high = lax.ppermute(own, "space", back)
        if c >= 1:
            low, high, part = lax.optimization_barrier((low, high, part))
            if received:
                part, received[-1] = lax.optimization_barrier((part, received[-1]))
            received.append(lax.all_to_all(part, "block", 0, 0, tiled=True))
        if c == 0:
            part, terms = filtered(low, own, high, blocks, scales=scales)
        else:
            part = filtered(low, own, high, blocks, terms=terms)
    part, received[-1] = lax.optimization_barrier((part, received[-1]))
    received.append(lax.all_to_all(part, "block", 0, 0, tiled=True))
    devices = blocks * slabs
    pieces = partial_gram(received, devices)
    summed = jnp.sum(lax.all_to_all(pieces, ("space", "block"), 0, 0, tiled=True), axis=0)
    gram = lax.all_to_all(
        jnp.broadcast_to(summed[None], pieces.shape), ("space", "block"), 0, 0, tiled=True
    ).reshape(rank, rank)
    inverse = inverse_factor(gram, 1.0 / cells)
    result = product(inverse, received)
    sent = lax.all_to_all(result, "block", 0, 0, tiled=True)
    return assembled(sent.reshape(planes, halves, per_device, width))


def solution(mesh):
    return jax.shard_map(
        local,
        mesh=mesh,
        in_specs=(P("block", "space", None), P("space", None), P()),
        out_specs=P("block", "space", None),
        check_vma=False,
    )
```

```python
import functools
import math

import jax
import jax.numpy as jnp
from jax import lax
from jax.experimental import pallas as pl
from jax.experimental.pallas import tpu as pltpu
from jax.sharding import PartitionSpec as P

NZ = 96
DEGREE = 4
LANES = 128
CHUNK = 8
PANEL = 64
BLOCK = 18 * LANES
HIGHEST = lax.Precision.HIGHEST


def neighbours(axis):
    count = lax.axis_size(axis)
    up = [(i, i + 1) for i in range(count - 1)]
    return up, [(b, a) for a, b in up]


def first_chunk_kernel(table, labels, vectors, out):
    out[0:CHUNK] = vectors[...]
    phase = labels[...]
    out[CHUNK] = jnp.where(phase == 0, table[0], jnp.where(phase == 1, table[1], table[2]))


def first_chunk(vectors, labels, table):
    planes, cells = labels.shape
    return pl.pallas_call(
        first_chunk_kernel,
        grid=(1,),
        out_shape=jax.ShapeDtypeStruct((CHUNK + 1, planes, cells), jnp.float32),
        in_specs=[
            pl.BlockSpec(memory_space=pltpu.SMEM),
            pl.BlockSpec((planes, cells), lambda i: (0, 0)),
            pl.BlockSpec((CHUNK, planes, cells), lambda i: (0, 0, 0)),
        ],
        out_specs=pl.BlockSpec((CHUNK + 1, planes, cells), lambda i: (0, 0, 0)),
        name="first_chunk",
    )(table, labels, vectors)


def face(left_k, right_k):
    filled = jnp.where(right_k > 0, right_k, left_k)
    return 2.0 * left_k * filled / (left_k + filled)


def terms_kernel(planes, scales, raw, out, window):
    scale, shift = scales[0], scales[1]
    count = out.shape[0]
    window[...] = jnp.zeros_like(window)
    for k in range(3):
        window[k * planes : (k + 1) * planes, :] = raw[k, CHUNK]
    cells = window.shape[1]
    span = 3 * LANES * NZ // math.gcd(3 * LANES, NZ)
    assert cells % span == 0
    z = lax.rem(lax.broadcasted_iota(jnp.int32, (8, span), 1), NZ)

    def body(g, carry):
        lanes = pl.ds(pl.multiple_of(g * span, span), span)
        left = pl.ds(pl.multiple_of(jnp.maximum(g * span - LANES, 0), LANES), LANES)
        right = pl.ds(
            pl.multiple_of(jnp.minimum(g * span + span, cells - LANES), LANES), LANES
        )
        for base in range(0, count, 8):
            rows = pl.ds(base + 1, 8)
            kappa = window[rows, lanes]
            inside = kappa > 0
            safe = jnp.where(inside, kappa, 1.0)
            before = jnp.where(g == 0, 0.0, window[rows, left])
            after = jnp.where(g * span + span == cells, 0.0, window[rows, right])
            wide = jnp.concatenate([before, kappa, after], axis=1)
            total = wide.shape[1]

            def moved(offset):
                return pltpu.roll(wide, (-offset) % total, 1)[:, LANES : LANES + span]

            around = [
                window[pl.ds(base, 8), lanes],
                window[pl.ds(base + 2, 8), lanes],
                jnp.where(z < NZ - 1, moved(1), 0.0),
                jnp.where(z > 0, moved(-1), 0.0),
                moved(NZ),
                moved(-NZ),
            ]
            faces = [face(safe, k) for k in around]
            diagonal = functools.reduce(jnp.add, faces) - shift
            values = [jnp.where(inside, diagonal * scale, 0.0)]
            for f, k in zip(faces, around):
                values.append(jnp.where(inside & (k > 0), -scale * f, 0.0))
            kept = min(8, count - base)
            for k, value in enumerate(values):
                out[base : base + kept, k, lanes] = value[:kept]
        return carry

    lax.fori_loop(0, cells // span, body, 0)


def halved(value):
    high = value.astype(jnp.bfloat16)
    return high, (value - high.astype(jnp.float32)).astype(jnp.bfloat16)


def dot(left, right):
    return jnp.dot(left, right, preferred_element_type=jnp.float32)


def start_reading(sources, raw, sems):
    copies = [
        pltpu.make_async_copy(source, raw.at[k], sems.at[k]) for k, source in enumerate(sources)
    ]
    for copy in copies:
        copy.start()
    return copies


def filter_kernel(planes, halves, arriving, raw, terms, target_array, out, sems, y0, y1, y2, y3, turn):
    for k in range(3):
        if k < len(arriving):
            arriving[k].wait()
        for p in range(planes):
            y0[k * planes + p] = raw[k, 0:CHUNK, p, :]
    for copy in arriving[3:]:
        copy.wait()
    cells = y0.shape[-1]
    tiles = cells // LANES
    per_half = tiles // halves
    lane = lax.broadcasted_iota(jnp.int32, (CHUNK, LANES), 1)
    last, first = lane == LANES - 1, lane == 0
    source_lane = lax.broadcasted_iota(jnp.int32, turn.shape, 0) % LANES
    to = lax.broadcasted_iota(jnp.int32, turn.shape, 1)
    wanted = lax.rem(to + jnp.where(to < LANES, 1, LANES - 1), LANES)
    turn[...] = jnp.where(source_lane == wanted, 1.0, 0.0).astype(jnp.bfloat16)
    head, tail = lane < NZ, lane >= LANES - NZ

    def sweep(source, source_at, previous, previous_at, target, at, half_step):
        count = target_planes(target)

        def plane_body(p, carry):
            w = p + at

            s = source_at(w)

            def tile(array, plane, t):
                return array[plane, :, t * LANES : (t + 1) * LANES]

            turned = dot(
                jnp.concatenate(
                    halved(jnp.concatenate([tile(source, s, t) for t in range(tiles)], axis=0)),
                    axis=1,
                ),
                turn[...],
            )

            def moved(t, way):
                t = t % tiles
                return turned[CHUNK * t : CHUNK * (t + 1), way * LANES : (way + 1) * LANES]

            row = [tile(source, s, tiles - 1), tile(source, s, 0)]
            for t in range(tiles):
                left, here = row
                right = tile(source, s, (t + 1) % tiles)
                row = [here, right]
                term = [terms[w - 1, k : k + 1, t * LANES : (t + 1) * LANES] for k in range(7)]
                total = term[0] * here
                total += term[1] * tile(source, s - 1, t)
                total += term[2] * tile(source, s + 1, t)
                total += term[3] * jnp.where(last, moved(t + 1, 0), moved(t, 0))
                total += term[4] * jnp.where(first, moved(t - 1, 1), moved(t, 1))
                total += term[5] * pltpu.roll(jnp.where(head, right, here), LANES - NZ, 1)
                total += term[6] * pltpu.roll(jnp.where(tail, left, here), NZ, 1)
                total = 0.5 * total if half_step else total - tile(previous, previous_at(w), t)
                if target is out:
                    inner = t % per_half * LANES
                    out[p * halves + t // per_half, :, inner : inner + LANES] = total
                else:
                    target[p, :, t * LANES : (t + 1) * LANES] = total
            if target is out:
                leaving(p).start()
            return carry

        lax.fori_loop(0, count, plane_body, 0)

    def target_planes(target):
        return planes if target is out else target.shape[0]

    def leaving(p):
        rows = pl.ds(p * halves, halves)
        return pltpu.make_async_copy(out.at[rows], target_array.at[rows], sems.at[p])

    sweep(y0, lambda w: w, None, None, y1, 1, True)
    sweep(y1, lambda w: w - 1, y0, lambda w: w, y2, 2, False)
    sweep(y2, lambda w: w - 2, y1, lambda w: w - 1, y3, 3, False)
    sweep(y3, lambda w: w - 3, y2, lambda w: w - 2, out, 4, False)
    for p in range(planes):
        leaving(p).wait()


def next_filter_kernel(
    planes, halves, low, own, high, stored, target, raw, sems, out, y0, y1, y2, y3, terms, turn
):
    copies = start_reading((low, own, high), raw, sems)
    last = pltpu.make_async_copy(stored, terms, sems.at[3 + planes])
    last.start()
    filter_kernel(
        planes, halves, (*copies, last), raw, terms, target, out, sems.at[pl.ds(3, planes)], y0, y1, y2, y3,
        turn,
    )


def first_filter_kernel(
    planes, halves, scales, low, own, high, target, stored, raw, sems, out, y0, y1, y2, y3, terms, turn,
    window,
):
    for copy in start_reading((low, own, high), raw, sems):
        copy.wait()
    terms_kernel(planes, scales, raw, terms, window)
    last = pltpu.make_async_copy(terms, stored, sems.at[3 + planes])
    last.start()
    filter_kernel(
        planes, halves, (), raw, terms, target, out, sems.at[pl.ds(3, planes)], y0, y1, y2, y3,
        turn,
    )
    last.wait()


def filtered(low, own, high, blocks, terms=None, scales=None):
    rows, planes, cells = own.shape
    halves = blocks // planes
    width = cells // halves
    steps = (3 * planes, 3 * planes - 2, 3 * planes - 4, 3 * planes - 6)
    hbm = pl.BlockSpec(memory_space=pltpu.HBM)
    part = jax.ShapeDtypeStruct((blocks, CHUNK, width), jnp.float32)
    scratch = [
        pltpu.VMEM((3, rows, planes, cells), jnp.float32),
        pltpu.SemaphoreType.DMA((4 + planes,)),
        pltpu.VMEM(part.shape, jnp.float32),
    ]
    scratch += [pltpu.VMEM((count, CHUNK, cells), jnp.float32) for count in steps]
    factors = jax.ShapeDtypeStruct((3 * planes - 2, 8, cells), jnp.float32)
    scratch.append(pltpu.VMEM(factors.shape, jnp.float32))
    scratch.append(pltpu.VMEM((2 * LANES, 2 * LANES), jnp.bfloat16))
    options = dict(
        compiler_params=pltpu.CompilerParams(vmem_limit_bytes=60 * 2**20),
        cost_estimate=pl.CostEstimate(
            flops=14 * 7 * planes * CHUNK * cells,
            bytes_accessed=4 * 44 * CHUNK * cells,
            transcendentals=0,
        ),
    )
    if scales is None:
        return pl.pallas_call(
            functools.partial(next_filter_kernel, planes, halves),
            out_shape=part,
            in_specs=[hbm] * 4,
            out_specs=hbm,
            scratch_shapes=scratch,
            name="chebyshev",
            **options,
        )(low, own, high, terms)
    return pl.pallas_call(
        functools.partial(first_filter_kernel, planes, halves),
        out_shape=[part, factors],
        in_specs=[pl.BlockSpec(memory_space=pltpu.SMEM)] + [hbm] * 3,
        out_specs=[hbm] * 2,
        scratch_shapes=scratch + [pltpu.VMEM((24, cells), jnp.float32)],
        name="first_chebyshev",
        **options,
    )(scales, low, own, high)


def rows_in_order(chunks):
    blocks = chunks[0].shape[0]
    return jnp.concatenate([c[b] for b in range(blocks) for c in chunks], axis=0)


def gram_kernel(*refs):
    *chunks, out, cross = refs
    step = pl.program_id(0)
    rank = cross.shape[0]
    high, low = halved(rows_in_order(chunks))

    def inner(left, right):
        return lax.dot_general(
            left, right, (((1,), (1,)), ((), ())), preferred_element_type=jnp.float32
        )

    square, mixed = inner(high, high).reshape(out.shape), inner(high, low)

    @pl.when(step == 0)
    def _():
        out[...] = square
        cross[...] = mixed

    @pl.when(step > 0)
    def _():
        out[...] += square
        cross[...] += mixed

    @pl.when(step == pl.num_programs(0) - 1)
    def _():
        both = cross[...] + jnp.transpose(cross[...])
        out[...] += both.reshape(out.shape)


def partial_gram(chunks, pieces):
    blocks, rows, width = chunks[0].shape
    rank = blocks * rows * len(chunks)
    shape = (pieces, rank // pieces, rank)
    return pl.pallas_call(
        gram_kernel,
        grid=(width // BLOCK,),
        out_shape=jax.ShapeDtypeStruct(shape, jnp.float32),
        in_specs=[pl.BlockSpec((blocks, rows, BLOCK), lambda i: (0, 0, i))] * len(chunks),
        out_specs=pl.BlockSpec(shape, lambda i: (0, 0, 0)),
        scratch_shapes=[pltpu.VMEM((rank, rank), jnp.float32)],
        compiler_params=pltpu.CompilerParams(vmem_limit_bytes=60 * 2**20),
        name="partial_gram",
    )(*chunks)


def product_kernel(inverse, *refs):
    *chunks, out = refs
    (a, b), (x, y) = halved(inverse[...]), halved(rows_in_order(chunks))
    out[...] = (dot(a, x) + (dot(a, y) + dot(b, x))).reshape(out.shape)


def product(inverse, chunks):
    blocks, rows, width = chunks[0].shape
    rank = inverse.shape[0]
    return pl.pallas_call(
        product_kernel,
        grid=(width // BLOCK,),
        out_shape=jax.ShapeDtypeStruct((blocks, rank // blocks, width), jnp.float32),
        in_specs=[pl.BlockSpec((rank, rank), lambda i: (0, 0))]
        + [pl.BlockSpec((blocks, rows, BLOCK), lambda i: (0, 0, i))] * len(chunks),
        out_specs=pl.BlockSpec((blocks, rank // blocks, BLOCK), lambda i: (0, 0, i)),
        compiler_params=pltpu.CompilerParams(vmem_limit_bytes=60 * 2**20),
        name="product",
    )(inverse, *chunks)


def assemble_kernel(planes, source, out):
    for m in range(0, out.shape[0], 8):
        for p in range(planes):
            out[m : m + 8, p, :] = source[p, 0, m : m + 8, :]


def assembled(pieces):
    planes, halves, rows, width = pieces.shape
    return pl.pallas_call(
        functools.partial(assemble_kernel, planes),
        grid=(halves,),
        out_shape=jax.ShapeDtypeStruct((rows, planes, halves * width), jnp.float32),
        in_specs=[pl.BlockSpec((planes, 1, rows, width), lambda i: (0, i, 0, 0))],
        out_specs=pl.BlockSpec((rows, planes, width), lambda i: (0, 0, i)),
        compiler_params=pltpu.CompilerParams(vmem_limit_bytes=32 * 2**20),
        name="assemble",
    )(pieces)


def inverse_factor_kernel(scale, gram, out, work):
    rank = gram.shape[0]
    work[...] = gram[...] * scale
    lane = lax.broadcasted_iota(jnp.int32, (8, LANES), 1)
    sub = lax.broadcasted_iota(jnp.int32, (8, LANES), 0)
    wide = (8, LANES)
    parts = rank // LANES
    count = PANEL // 8
    for k0 in range(0, rank, PANEL):
        groups = [
            [work[k0 + 8 * g : k0 + 8 * g + 8, LANES * h : LANES * h + LANES] for h in range(parts)]
            for g in range(count)
        ]
        pivots = []
        for at in range(count):
            first = k0 + 8 * at
            home, start = first // LANES, first % LANES
            spread = {
                g: [
                    jnp.broadcast_to(groups[g][home][:, start + j : start + j + 1], wide)
                    for j in range(8)
                ]
                for g in range(at, count)
            }
            kept_pivots = jnp.ones(wide, jnp.float32)
            for j in range(8):
                pivot = jnp.broadcast_to(spread[at][j][j : j + 1, :], wide)
                inverse = 1.0 / pivot
                kept_pivots = jnp.where(sub == j, pivot, kept_pivots)
                here = lane == start + j
                rows = [jnp.broadcast_to(v[j : j + 1, :], wide) for v in groups[at]]
                rows[home] = jnp.where(here, 1.0, rows[home])
                later = {
                    i: jnp.broadcast_to(spread[at][i][j : j + 1, :], wide) for i in range(j + 1, 8)
                }
                for g in range(at, count):
                    factor = spread[g][j] * inverse
                    kept = list(groups[g])
                    if g == at:
                        factor = jnp.where(sub > j, factor, 0.0)
                        kept[home] = jnp.where(
                            here & (sub >= j), jnp.where(sub == j, 1.0, 0.0), kept[home]
                        )
                    else:
                        kept[home] = jnp.where(here, 0.0, kept[home])
                    groups[g] = [v - factor * r for v, r in zip(kept, rows)]
                    for i in range(j + 1, 8):
                        spread[g][i] = spread[g][i] - factor * later[i]
            pivots.append(1.0 / jnp.sqrt(kept_pivots))
        panel = jnp.concatenate(
            [
                jnp.concatenate([v * p for v in group], axis=1)
                for group, p in zip(groups, pivots)
            ],
            axis=0,
        )
        done = k0 + PANEL
        columns = lax.broadcasted_iota(jnp.int32, (PANEL, rank), 1)
        rows = k0 + lax.broadcasted_iota(jnp.int32, (PANEL, rank), 0)
        behind = columns <= rows
        out[k0:done, :] = jnp.where(behind, panel, 0.0)
        panel = jnp.where(behind | (columns >= done), panel, 0.0)
        if done < rank:
            update = lax.dot_general(
                panel, panel, (((0,), (0,)), ((), ())), precision=HIGHEST,
                preferred_element_type=jnp.float32,
            )
            inside = (columns[:1] >= k0) & (columns[:1] < done)
            work[done:, :] = jnp.where(inside, 0.0, work[done:, :]) - update[done:, :]


def inverse_factor(gram, scale):
    rank = gram.shape[0]
    return pl.pallas_call(
        functools.partial(inverse_factor_kernel, scale),
        out_shape=jax.ShapeDtypeStruct((rank, rank), jnp.float32),
        in_specs=[pl.BlockSpec(memory_space=pltpu.VMEM)],
        out_specs=pl.BlockSpec(memory_space=pltpu.VMEM),
        scratch_shapes=[pltpu.VMEM((rank, rank), jnp.float32)],
        name="inverse_factor",
    )(gram)


def local(start_vectors, phase_labels, phase_conductivity):
    upper_bound = 12.0 * jnp.max(phase_conductivity)
    lower_bound = upper_bound / 10.0
    centre = (upper_bound + lower_bound) / 2.0
    radius = (upper_bound - lower_bound) / 2.0
    per_device, planes, plane_cells = start_vectors.shape
    blocks, slabs = lax.axis_size("block"), lax.axis_size("space")
    assert planes == DEGREE and blocks % planes == 0
    halves = blocks // planes
    width = plane_cells // halves
    cells = planes * slabs * plane_cells
    rank = per_device * blocks
    up, back = neighbours("space")
    chunks = per_device // CHUNK

    scales = jnp.stack([2.0 / radius, centre])
    received = []
    for c in range(chunks):
        if c == 0:
            own = first_chunk(start_vectors, phase_labels, phase_conductivity)
        else:
            own = start_vectors[c * CHUNK : (c + 1) * CHUNK]
        low = lax.ppermute(own, "space", up)
        high = lax.ppermute(own, "space", back)
        if c >= 1:
            low, high, _ = lax.optimization_barrier((low, high, part))
            if received:
                part, received[-1] = lax.optimization_barrier((part, received[-1]))
            received.append(lax.all_to_all(part, "block", 0, 0, tiled=True))
        if c == 0:
            part, terms = filtered(low, own, high, blocks, scales=scales)
        else:
            part = filtered(low, own, high, blocks, terms=terms)
    part, received[-1] = lax.optimization_barrier((part, received[-1]))
    received.append(lax.all_to_all(part, "block", 0, 0, tiled=True))
    devices = blocks * slabs
    pieces = partial_gram(received, devices)
    summed = jnp.sum(lax.all_to_all(pieces, ("space", "block"), 0, 0, tiled=True), axis=0)
    gram = lax.all_to_all(
        jnp.broadcast_to(summed[None], pieces.shape), ("space", "block"), 0, 0, tiled=True
    ).reshape(rank, rank)
    inverse = inverse_factor(gram, 1.0 / cells)
    result = product(inverse, received)
    sent = lax.all_to_all(result, "block", 0, 0, tiled=True)
    return assembled(sent.reshape(planes, halves, per_device, width))


def solution(mesh):
    return jax.shard_map(
        local,
        mesh=mesh,
        in_specs=(P("block", "space", None), P("space", None), P()),
        out_specs=P("block", "space", None),
        check_vma=False,
    )
```

```python
import functools
import math

import jax
import jax.numpy as jnp
from jax import lax
from jax.experimental import pallas as pl
from jax.experimental.pallas import tpu as pltpu
from jax.sharding import PartitionSpec as P

NZ = 96
DEGREE = 4
LANES = 128
CHUNK = 8
PANEL = 64
BLOCK = 18 * LANES
HIGHEST = lax.Precision.HIGHEST


def neighbours(axis):
    count = lax.axis_size(axis)
    up = [(i, i + 1) for i in range(count - 1)]
    return up, [(b, a) for a, b in up]


def first_chunk_kernel(table, labels, vectors, out):
    out[0:CHUNK] = vectors[...]
    phase = labels[...]
    out[CHUNK] = jnp.where(phase == 0, table[0], jnp.where(phase == 1, table[1], table[2]))


def first_chunk(vectors, labels, table):
    planes, cells = labels.shape
    return pl.pallas_call(
        first_chunk_kernel,
        grid=(1,),
        out_shape=jax.ShapeDtypeStruct((CHUNK + 1, planes, cells), jnp.float32),
        in_specs=[
            pl.BlockSpec(memory_space=pltpu.SMEM),
            pl.BlockSpec((planes, cells), lambda i: (0, 0)),
            pl.BlockSpec((CHUNK, planes, cells), lambda i: (0, 0, 0)),
        ],
        out_specs=pl.BlockSpec((CHUNK + 1, planes, cells), lambda i: (0, 0, 0)),
        name="first_chunk",
    )(table, labels, vectors)


def face(left_k, right_k):
    filled = jnp.where(right_k > 0, right_k, left_k)
    return 2.0 * left_k * filled / (left_k + filled)


def terms_kernel(planes, scales, raw, out, window):
    scale, shift = scales[0], scales[1]
    count = out.shape[0]
    window[...] = jnp.zeros_like(window)
    for k in range(3):
        window[k * planes : (k + 1) * planes, :] = raw[k, CHUNK]
    cells = window.shape[1]
    span = 3 * LANES * NZ // math.gcd(3 * LANES, NZ)
    assert cells % span == 0
    z = lax.rem(lax.broadcasted_iota(jnp.int32, (8, span), 1), NZ)

    def body(g, carry):
        lanes = pl.ds(pl.multiple_of(g * span, span), span)
        left = pl.ds(pl.multiple_of(jnp.maximum(g * span - LANES, 0), LANES), LANES)
        right = pl.ds(
            pl.multiple_of(jnp.minimum(g * span + span, cells - LANES), LANES), LANES
        )
        for base in range(0, count, 8):
            rows = pl.ds(base + 1, 8)
            kappa = window[rows, lanes]
            inside = kappa > 0
            safe = jnp.where(inside, kappa, 1.0)
            before = jnp.where(g == 0, 0.0, window[rows, left])
            after = jnp.where(g * span + span == cells, 0.0, window[rows, right])
            wide = jnp.concatenate([before, kappa, after], axis=1)
            total = wide.shape[1]

            def moved(offset):
                return pltpu.roll(wide, (-offset) % total, 1)[:, LANES : LANES + span]

            around = [
                window[pl.ds(base, 8), lanes],
                window[pl.ds(base + 2, 8), lanes],
                jnp.where(z < NZ - 1, moved(1), 0.0),
                jnp.where(z > 0, moved(-1), 0.0),
                moved(NZ),
                moved(-NZ),
            ]
            faces = [face(safe, k) for k in around]
            diagonal = functools.reduce(jnp.add, faces) - shift
            values = [jnp.where(inside, diagonal * scale, 0.0)]
            for f, k in zip(faces, around):
                values.append(jnp.where(inside & (k > 0), -scale * f, 0.0))
            kept = min(8, count - base)
            for k, value in enumerate(values):
                out[base : base + kept, k, lanes] = value[:kept]
        return carry

    lax.fori_loop(0, cells // span, body, 0)


def halved(value):
    high = value.astype(jnp.bfloat16)
    return high, (value - high.astype(jnp.float32)).astype(jnp.bfloat16)


def dot(left, right):
    return jnp.dot(left, right, preferred_element_type=jnp.float32)


def start_reading(sources, raw, sems):
    copies = [
        pltpu.make_async_copy(source, raw.at[k], sems.at[k]) for k, source in enumerate(sources)
    ]
    for copy in copies:
        copy.start()
    return copies


def filter_kernel(planes, halves, arriving, raw, terms, target_array, out, sems, y0, y1, y2, y3, turn):
    for k in range(3):
        if k < len(arriving):
            arriving[k].wait()
        for p in range(planes):
            y0[k * planes + p] = raw[k, 0:CHUNK, p, :]
    for copy in arriving[3:]:
        copy.wait()
    cells = y0.shape[-1]
    tiles = cells // LANES
    per_half = tiles // halves
    lane = lax.broadcasted_iota(jnp.int32, (CHUNK, LANES), 1)
    last, first = lane == LANES - 1, lane == 0
    source_lane = lax.broadcasted_iota(jnp.int32, turn.shape, 0) % LANES
    to = lax.broadcasted_iota(jnp.int32, turn.shape, 1)
    wanted = lax.rem(to + jnp.where(to < LANES, 1, LANES - 1), LANES)
    turn[...] = jnp.where(source_lane == wanted, 1.0, 0.0).astype(jnp.bfloat16)
    head, tail = lane < NZ, lane >= LANES - NZ

    def sweep(source, source_at, previous, previous_at, target, at, half_step):
        count = target_planes(target)

        def plane_body(p, carry):
            w = p + at

            s = source_at(w)

            def tile(array, plane, t):
                return array[plane, :, t * LANES : (t + 1) * LANES]

            turned = dot(
                jnp.concatenate(
                    halved(jnp.concatenate([tile(source, s, t) for t in range(tiles)], axis=0)),
                    axis=1,
                ),
                turn[...],
            )

            def moved(t, way):
                t = t % tiles
                return turned[CHUNK * t : CHUNK * (t + 1), way * LANES : (way + 1) * LANES]

            row = [tile(source, s, tiles - 1), tile(source, s, 0)]
            for t in range(tiles):
                left, here = row
                right = tile(source, s, (t + 1) % tiles)
                row = [here, right]
                term = [terms[w - 1, k : k + 1, t * LANES : (t + 1) * LANES] for k in range(7)]
                total = term[0] * here
                total += term[1] * tile(source, s - 1, t)
                total += term[2] * tile(source, s + 1, t)
                total += term[3] * jnp.where(last, moved(t + 1, 0), moved(t, 0))
                total += term[4] * jnp.where(first, moved(t - 1, 1), moved(t, 1))
                total += term[5] * pltpu.roll(jnp.where(head, right, here), LANES - NZ, 1)
                total += term[6] * pltpu.roll(jnp.where(tail, left, here), NZ, 1)
                total = 0.5 * total if half_step else total - tile(previous, previous_at(w), t)
                if target is out:
                    inner = t % per_half * LANES
                    out[p * halves + t // per_half, :, inner : inner + LANES] = total
                else:
                    target[p, :, t * LANES : (t + 1) * LANES] = total
            if target is out:
                leaving(p).start()
            return carry

        lax.fori_loop(0, count, plane_body, 0)

    def target_planes(target):
        return planes if target is out else target.shape[0]

    def leaving(p):
        rows = pl.ds(p * halves, halves)
        return pltpu.make_async_copy(out.at[rows], target_array.at[rows], sems.at[p])

    sweep(y0, lambda w: w, None, None, y1, 1, True)
    sweep(y1, lambda w: w - 1, y0, lambda w: w, y2, 2, False)
    sweep(y2, lambda w: w - 2, y1, lambda w: w - 1, y3, 3, False)
    sweep(y3, lambda w: w - 3, y2, lambda w: w - 2, out, 4, False)
    for p in range(planes):
        leaving(p).wait()


def next_filter_kernel(
    planes, halves, low, own, high, stored, target, raw, sems, out, y0, y1, y2, y3, terms, turn
):
    copies = start_reading((low, own, high), raw, sems)
    last = pltpu.make_async_copy(stored, terms, sems.at[3 + planes])
    last.start()
    filter_kernel(
        planes, halves, (*copies, last), raw, terms, target, out, sems.at[pl.ds(3, planes)], y0, y1, y2, y3,
        turn,
    )


def first_filter_kernel(
    planes, halves, scales, low, own, high, target, stored, raw, sems, out, y0, y1, y2, y3, terms, turn,
    window,
):
    for copy in start_reading((low, own, high), raw, sems):
        copy.wait()
    terms_kernel(planes, scales, raw, terms, window)
    last = pltpu.make_async_copy(terms, stored, sems.at[3 + planes])
    last.start()
    filter_kernel(
        planes, halves, (), raw, terms, target, out, sems.at[pl.ds(3, planes)], y0, y1, y2, y3,
        turn,
    )
    last.wait()


def filtered(low, own, high, blocks, terms=None, scales=None):
    rows, planes, cells = own.shape
    halves = blocks // planes
    width = cells // halves
    steps = (3 * planes, 3 * planes - 2, 3 * planes - 4, 3 * planes - 6)
    hbm = pl.BlockSpec(memory_space=pltpu.HBM)
    part = jax.ShapeDtypeStruct((blocks, CHUNK, width), jnp.float32)
    scratch = [
        pltpu.VMEM((3, rows, planes, cells), jnp.float32),
        pltpu.SemaphoreType.DMA((4 + planes,)),
        pltpu.VMEM(part.shape, jnp.float32),
    ]
    scratch += [pltpu.VMEM((count, CHUNK, cells), jnp.float32) for count in steps]
    factors = jax.ShapeDtypeStruct((3 * planes - 2, 8, cells), jnp.float32)
    scratch.append(pltpu.VMEM(factors.shape, jnp.float32))
    scratch.append(pltpu.VMEM((2 * LANES, 2 * LANES), jnp.bfloat16))
    options = dict(
        compiler_params=pltpu.CompilerParams(vmem_limit_bytes=60 * 2**20),
        cost_estimate=pl.CostEstimate(
            flops=14 * 7 * planes * CHUNK * cells,
            bytes_accessed=4 * 44 * CHUNK * cells,
            transcendentals=0,
        ),
    )
    if scales is None:
        return pl.pallas_call(
            functools.partial(next_filter_kernel, planes, halves),
            out_shape=part,
            in_specs=[hbm] * 4,
            out_specs=hbm,
            scratch_shapes=scratch,
            name="chebyshev",
            **options,
        )(low, own, high, terms)
    return pl.pallas_call(
        functools.partial(first_filter_kernel, planes, halves),
        out_shape=[part, factors],
        in_specs=[pl.BlockSpec(memory_space=pltpu.SMEM)] + [hbm] * 3,
        out_specs=[hbm] * 2,
        scratch_shapes=scratch + [pltpu.VMEM((24, cells), jnp.float32)],
        name="first_chebyshev",
        **options,
    )(scales, low, own, high)


def rows_in_order(chunks):
    blocks = chunks[0].shape[0]
    return jnp.concatenate([c[b] for b in range(blocks) for c in chunks], axis=0)


def gram_kernel(*refs):
    *chunks, out, cross = refs
    step = pl.program_id(0)
    rank = cross.shape[0]
    high, low = halved(rows_in_order(chunks))

    def inner(left, right):
        return lax.dot_general(
            left, right, (((1,), (1,)), ((), ())), preferred_element_type=jnp.float32
        )

    square, mixed = inner(high, high).reshape(out.shape), inner(high, low)

    @pl.when(step == 0)
    def _():
        out[...] = square
        cross[...] = mixed

    @pl.when(step > 0)
    def _():
        out[...] += square
        cross[...] += mixed

    @pl.when(step == pl.num_programs(0) - 1)
    def _():
        both = cross[...] + jnp.transpose(cross[...])
        out[...] += both.reshape(out.shape)


def partial_gram(chunks, pieces):
    blocks, rows, width = chunks[0].shape
    rank = blocks * rows * len(chunks)
    shape = (pieces, rank // pieces, rank)
    return pl.pallas_call(
        gram_kernel,
        grid=(width // BLOCK,),
        out_shape=jax.ShapeDtypeStruct(shape, jnp.float32),
        in_specs=[pl.BlockSpec((blocks, rows, BLOCK), lambda i: (0, 0, i))] * len(chunks),
        out_specs=pl.BlockSpec(shape, lambda i: (0, 0, 0)),
        scratch_shapes=[pltpu.VMEM((rank, rank), jnp.float32)],
        compiler_params=pltpu.CompilerParams(vmem_limit_bytes=60 * 2**20),
        name="partial_gram",
    )(*chunks)


def product_kernel(inverse, *refs):
    *chunks, out = refs
    (a, b), (x, y) = halved(inverse[...]), halved(rows_in_order(chunks))
    out[...] = (dot(a, x) + (dot(a, y) + dot(b, x))).reshape(out.shape)


def product(inverse, chunks):
    blocks, rows, width = chunks[0].shape
    rank = inverse.shape[0]
    return pl.pallas_call(
        product_kernel,
        grid=(width // BLOCK,),
        out_shape=jax.ShapeDtypeStruct((blocks, rank // blocks, width), jnp.float32),
        in_specs=[pl.BlockSpec((rank, rank), lambda i: (0, 0))]
        + [pl.BlockSpec((blocks, rows, BLOCK), lambda i: (0, 0, i))] * len(chunks),
        out_specs=pl.BlockSpec((blocks, rank // blocks, BLOCK), lambda i: (0, 0, i)),
        compiler_params=pltpu.CompilerParams(vmem_limit_bytes=32 * 2**20),
        name="product",
    )(inverse, *chunks)


def assemble_kernel(planes, source, out):
    for m in range(0, out.shape[0], 8):
        for p in range(planes):
            out[m : m + 8, p, :] = source[p, 0, m : m + 8, :]


def assembled(pieces):
    planes, halves, rows, width = pieces.shape
    return pl.pallas_call(
        functools.partial(assemble_kernel, planes),
        grid=(halves,),
        out_shape=jax.ShapeDtypeStruct((rows, planes, halves * width), jnp.float32),
        in_specs=[pl.BlockSpec((planes, 1, rows, width), lambda i: (0, i, 0, 0))],
        out_specs=pl.BlockSpec((rows, planes, width), lambda i: (0, 0, i)),
        compiler_params=pltpu.CompilerParams(vmem_limit_bytes=32 * 2**20),
        name="assemble",
    )(pieces)


def inverse_factor_kernel(scale, gram, out, work):
    rank = gram.shape[0]
    work[...] = gram[...] * scale
    lane = lax.broadcasted_iota(jnp.int32, (8, LANES), 1)
    sub = lax.broadcasted_iota(jnp.int32, (8, LANES), 0)
    wide = (8, LANES)
    parts = rank // LANES
    count = PANEL // 8
    for k0 in range(0, rank, PANEL):
        groups = [
            [work[k0 + 8 * g : k0 + 8 * g + 8, LANES * h : LANES * h + LANES] for h in range(parts)]
            for g in range(count)
        ]
        pivots = []
        for at in range(count):
            first = k0 + 8 * at
            home, start = first // LANES, first % LANES
            spread = {
                g: [
                    jnp.broadcast_to(groups[g][home][:, start + j : start + j + 1], wide)
                    for j in range(8)
                ]
                for g in range(at, count)
            }
            kept_pivots = jnp.ones(wide, jnp.float32)
            for j in range(8):
                pivot = jnp.broadcast_to(spread[at][j][j : j + 1, :], wide)
                inverse = 1.0 / pivot
                kept_pivots = jnp.where(sub == j, pivot, kept_pivots)
                here = lane == start + j
                rows = [jnp.broadcast_to(v[j : j + 1, :], wide) for v in groups[at]]
                rows[home] = jnp.where(here, 1.0, rows[home])
                later = {
                    i: jnp.broadcast_to(spread[at][i][j : j + 1, :], wide) for i in range(j + 1, 8)
                }
                for g in range(at, count):
                    factor = spread[g][j] * inverse
                    kept = list(groups[g])
                    if g == at:
                        factor = jnp.where(sub > j, factor, 0.0)
                        kept[home] = jnp.where(
                            here & (sub >= j), jnp.where(sub == j, 1.0, 0.0), kept[home]
                        )
                    else:
                        kept[home] = jnp.where(here, 0.0, kept[home])
                    groups[g] = [v - factor * r for v, r in zip(kept, rows)]
                    for i in range(j + 1, 8):
                        spread[g][i] = spread[g][i] - factor * later[i]
            pivots.append(1.0 / jnp.sqrt(kept_pivots))
        panel = jnp.concatenate(
            [
                jnp.concatenate([v * p for v in group], axis=1)
                for group, p in zip(groups, pivots)
            ],
            axis=0,
        )
        done = k0 + PANEL
        columns = lax.broadcasted_iota(jnp.int32, (PANEL, rank), 1)
        rows = k0 + lax.broadcasted_iota(jnp.int32, (PANEL, rank), 0)
        behind = columns <= rows
        out[k0:done, :] = jnp.where(behind, panel, 0.0)
        panel = jnp.where(behind | (columns >= done), panel, 0.0)
        if done < rank:
            update = lax.dot_general(
                panel, panel, (((0,), (0,)), ((), ())), precision=HIGHEST,
                preferred_element_type=jnp.float32,
            )
            inside = (columns[:1] >= k0) & (columns[:1] < done)
            work[done:, :] = jnp.where(inside, 0.0, work[done:, :]) - update[done:, :]


def inverse_factor(gram, scale):
    rank = gram.shape[0]
    return pl.pallas_call(
        functools.partial(inverse_factor_kernel, scale),
        out_shape=jax.ShapeDtypeStruct((rank, rank), jnp.float32),
        in_specs=[pl.BlockSpec(memory_space=pltpu.VMEM)],
        out_specs=pl.BlockSpec(memory_space=pltpu.VMEM),
        scratch_shapes=[pltpu.VMEM((rank, rank), jnp.float32)],
        name="inverse_factor",
    )(gram)


def local(start_vectors, phase_labels, phase_conductivity):
    upper_bound = 12.0 * jnp.max(phase_conductivity)
    lower_bound = upper_bound / 10.0
    centre = (upper_bound + lower_bound) / 2.0
    radius = (upper_bound - lower_bound) / 2.0
    per_device, planes, plane_cells = start_vectors.shape
    blocks, slabs = lax.axis_size("block"), lax.axis_size("space")
    assert planes == DEGREE and blocks % planes == 0
    halves = blocks // planes
    width = plane_cells // halves
    cells = planes * slabs * plane_cells
    rank = per_device * blocks
    up, back = neighbours("space")
    chunks = per_device // CHUNK

    scales = jnp.stack([2.0 / radius, centre])
    received = []
    for c in range(chunks):
        if c == 0:
            own = first_chunk(start_vectors, phase_labels, phase_conductivity)
        else:
            own = start_vectors[c * CHUNK : (c + 1) * CHUNK]
        low = lax.ppermute(own, "space", up)
        high = lax.ppermute(own, "space", back)
        if c >= 1:
            low, high, _ = lax.optimization_barrier((low, high, part))
            if received:
                part, received[-1] = lax.optimization_barrier((part, received[-1]))
            received.append(lax.all_to_all(part, "block", 0, 0, tiled=True))
        if c == 0:
            part, terms = filtered(low, own, high, blocks, scales=scales)
        else:
            part = filtered(low, own, high, blocks, terms=terms)
    part, received[-1] = lax.optimization_barrier((part, received[-1]))
    received.append(lax.all_to_all(part, "block", 0, 0, tiled=True))
    devices = blocks * slabs
    pieces = partial_gram(received, devices)
    summed = jnp.sum(lax.all_to_all(pieces, ("space", "block"), 0, 0, tiled=True), axis=0)
    gram = lax.all_to_all(
        jnp.broadcast_to(summed[None], pieces.shape), ("space", "block"), 0, 0, tiled=True
    ).reshape(rank, rank)
    inverse = inverse_factor(gram, 1.0 / cells)
    result = product(inverse, received)
    sent = lax.all_to_all(result, "block", 0, 0, tiled=True)
    return assembled(sent.reshape(planes, halves, per_device, width))


def solution(mesh):
    return jax.shard_map(
        local,
        mesh=mesh,
        in_specs=(P("block", "space", None), P("space", None), P()),
        out_specs=P("block", "space", None),
        check_vma=False,
    )
```
